256 devices in a mesh: sec: 4 (over z_hi, core), tile: 64 (over z_lo, y, x).
Axes of the slice: x: 4, y: 4, z: 8 (z_hi: 2, z_lo: 4; z = z_hi * 4 + z_lo), core: 2. Of those that a mesh axis runs over, the one named last changes fastest.
Arguments:
- sections: bfloat16 [4, 4096, 2048], P('sec', 'tile'), may hold values from -6 to 6
- earlier: bfloat16 [2, 4096, 2048], P(None, 'tile'), may hold values from -6 to 6
- offsets: int32 [4], P('sec'), may hold values from 1 to 2, as said below
- patch_valid: int32 [4, 64, 32], P('sec', 'tile'), may hold values 0 or 1
Outputs:
- node_flows: float32 [4, 2, 64, 32], P('sec', None, 'tile')
- confidence: float32 [4, 64, 32], P('sec', 'tile')
- positions: float32 [4, 2, 64, 32], P('sec', None, 'tile')
The draws below stay inside these ranges and needn't reach their ends.
Inputs may be any that keep to these rules, and one draw needn't show every extreme that they name: `offsets`: some section after the second takes 2, and another section after the first takes 1.
All inputs are finite; a program needn't handle non-finite values. No bound on the sum of `patch_valid` on one device may be relied on, other than what follows from the above.
Results may differ from the reference program's by a relative error of at most 0.0008.
Values may be sent and summed in bfloat16 or wider, within the bound.
No kernel may reach another device: no remote copies, remote signals or barrier semaphores. Data moves between devices by JAX's collectives and lax.ppermute only.
A program may use at most 64 MiB of HBM per device.

```python
import jax
import jax.numpy as jnp
from jax import lax

PATCH = 128
SPACING = 64
NODE_COLS = 32
STEPS = 3
SECTIONS = 4
NODE_ROWS = 64


def window_stack(key, amp_low, normal_part):
    drift_most = PATCH // 4
    jitter_most = PATCH // 16
    margin = drift_most + jitter_most + 1
    spacing = PATCH // 2
    row_total = NODE_ROWS * spacing
    col_total = NODE_COLS * spacing
    stack_count = SECTIONS + 2
    texture = jax.random.truncated_normal(jax.random.fold_in(key, 11), -4.0, 4.0, (row_total + 2 * margin, col_total + 2 * margin), jnp.float32)
    section_drift = jax.random.randint(jax.random.fold_in(key, 12), (stack_count, 1, 1, 2), -drift_most, drift_most + 1)
    jitter = jax.random.randint(jax.random.fold_in(key, 13), (stack_count, NODE_ROWS, NODE_COLS, 2), -jitter_most, jitter_most + 1)
    shifts = section_drift + jitter
    amplitude = jnp.exp(jax.random.uniform(jax.random.fold_in(key, 14), (stack_count, NODE_ROWS, NODE_COLS), jnp.float32, jnp.log(amp_low), 0.0))
    row_shift = jnp.repeat(jnp.repeat(shifts[..., 0], spacing, axis=1), spacing, axis=2)
    col_shift = jnp.repeat(jnp.repeat(shifts[..., 1], spacing, axis=1), spacing, axis=2)
    amp_full = jnp.repeat(jnp.repeat(amplitude, spacing, axis=1), spacing, axis=2)
    row_index = jnp.arange(row_total, dtype=jnp.int32)[None, :, None] + margin + row_shift
    col_index = jnp.arange(col_total, dtype=jnp.int32)[None, None, :] + margin + col_shift
    picked = texture[row_index, col_index]
    grain_noise = normal_part * jax.random.truncated_normal(jax.random.fold_in(key, 15), -4.0, 4.0, (stack_count, row_total, col_total), jnp.float32)
    return amp_full * picked + grain_noise


def draw_sections(key, part):
    stacked = window_stack(key, 0.05, 0.4)
    return stacked[2:].astype(jnp.bfloat16)


def draw_earlier(key, part):
    stacked = window_stack(key, 0.05, 0.4)
    return stacked[:2].astype(jnp.bfloat16)


def draw_offsets(key, part):
    key = jax.random.fold_in(key, 3)
    key_first = jax.random.fold_in(key, 1)
    key_second = jax.random.fold_in(key, 2)
    key_third = jax.random.fold_in(key, 4)
    first_draw = jax.random.randint(key_first, (SECTIONS,), 1, 3)
    slot_two = 2 + jax.random.randint(key_second, (), 0, SECTIONS - 2)
    slot_one = 1 + (slot_two + jax.random.randint(key_third, (), 0, SECTIONS - 2)) % (SECTIONS - 1)
    indices = jnp.arange(SECTIONS, dtype=jnp.int32)
    first_draw = jnp.where(indices == slot_two, 2, first_draw)
    first_draw = jnp.where(indices == slot_one, 1, first_draw)
    return first_draw.astype(jnp.int32)


def with_ends(values, key, low, largest):
    longest = values.shape.index(max(values.shape))
    spots = []
    for shift in (0, 1):
        where = [jax.random.randint(jax.random.fold_in(key, axis), (), 0, length) for axis, length in enumerate(values.shape)]
        where[longest] = (where[longest] + shift) % values.shape[longest]
        spots.append(tuple(where))
    return values.at[spots[0]].set(low).at[spots[1]].set(largest)


def setup_inputs(seed: int = 0) -> dict:
    splits = jax.random.split(jax.random.key(seed), 5)
    sections = draw_sections(jax.random.fold_in(splits[4], 71), 0)
    earlier = draw_earlier(jax.random.fold_in(splits[4], 71), 0)
    offsets = draw_offsets(jax.random.fold_in(splits[4], 71), 0)
    patch_valid = with_ends((jax.random.randint(splits[3], (SECTIONS, NODE_ROWS, NODE_COLS), 0, 8) < 7).astype(jnp.int32), jax.random.fold_in(splits[3], 1), 0, 1)
    return {"sections": sections, "earlier": earlier, "offsets": offsets, "patch_valid": patch_valid}


score_scale = 800.0
spring_rate = 0.3
plane_weight = 0.5

def node_windows(pixels, spacing):
    row_count = pixels.shape[0] // spacing - 1
    col_count = pixels.shape[1] // spacing - 1
    blocks = pixels.reshape(row_count + 1, spacing, col_count + 1, spacing)
    row_windows = jnp.concatenate([blocks[:-1], blocks[1:]], axis=1)
    return jnp.concatenate([row_windows[:, :, :-1], row_windows[:, :, 1:]], axis=3)

def displacement(length):
    indices = jnp.arange(length, dtype=jnp.int32)
    return jnp.where(indices < length // 2, indices, indices - length).astype(jnp.float32)

def patch_terms(current, previous):
    current = jnp.transpose(current, (1, 0, 2))
    previous = jnp.transpose(previous, (1, 0, 2))
    spectrum = jnp.fft.fft2(current) * jnp.conj(jnp.fft.fft2(previous))
    correlation = jnp.real(jnp.fft.ifft2(spectrum))
    energy = lax.optimization_barrier(jnp.sum(current * current, axis=(1, 2))) * lax.optimization_barrier(jnp.sum(previous * previous, axis=(1, 2)))
    scores = score_scale * correlation / jnp.sqrt(energy + 1e-06)[:, None, None]
    weights = jax.nn.softmax(scores, axis=(1, 2))
    shift_axis = displacement(current.shape[1])
    flow_rows = lax.optimization_barrier(jnp.sum(weights * shift_axis[None, :, None], axis=(1, 2)))
    flow_cols = lax.optimization_barrier(jnp.sum(weights * shift_axis[None, None, :], axis=(1, 2)))
    confidence = jax.scipy.special.logsumexp(scores, axis=(1, 2)) / score_scale
    return (jnp.stack([flow_rows, flow_cols]), confidence)

def reference(sections, earlier, offsets, patch_valid):
    rim_width = SPACING // 2
    prior_stack = jnp.concatenate([earlier, sections], axis=0)
    flow_list = []
    conf_list = []
    for section in range(SECTIONS):
        source = lax.dynamic_index_in_dim(prior_stack, (section + 2 - offsets[section]).astype(jnp.int32), 0, keepdims=False)
        current = jnp.pad(sections[section].astype(jnp.float32), rim_width)
        previous = jnp.pad(source.astype(jnp.float32), rim_width)

        def one_row(node_row):
            first_row = (node_row * SPACING).astype(jnp.int32)
            cur_rows = lax.dynamic_slice_in_dim(current, first_row, PATCH, 0)
            prev_rows = lax.dynamic_slice_in_dim(previous, first_row, PATCH, 0)
            return patch_terms(node_windows(cur_rows, SPACING)[0], node_windows(prev_rows, SPACING)[0])
        row_flows, row_conf = lax.map(one_row, jnp.arange(NODE_ROWS, dtype=jnp.int32))
        flow_list.append(jnp.transpose(row_flows, (1, 0, 2)))
        conf_list.append(row_conf)
    node_flows = jnp.stack(flow_list)
    confidence = jnp.stack(conf_list)
    stiffness = (patch_valid.astype(jnp.float32) * confidence)[:, None]
    one_mask = (offsets == 1).astype(jnp.float32)[:, None, None, None]
    two_mask = 1.0 - one_mask
    positions = jnp.zeros_like(node_flows)
    for iteration in range(STEPS):
        zero_slab = jnp.zeros_like(positions[:1])
        one_back = jnp.concatenate([zero_slab, positions[:-1]], axis=0)
        two_back = jnp.concatenate([zero_slab, zero_slab, positions[:-2]], axis=0)
        pulled = one_mask * one_back + two_mask * two_back
        tension = stiffness * (positions - pulled + node_flows)
        returned = jnp.concatenate([(one_mask * tension)[1:], zero_slab], axis=0) + jnp.concatenate([(two_mask * tension)[2:], zero_slab, zero_slab], axis=0)
        padded = jnp.pad(positions, ((0, 0), (0, 0), (1, 1), (1, 1)))
        bending = 4.0 * positions - padded[:, :, :-2, 1:-1] - padded[:, :, 2:, 1:-1] - padded[:, :, 1:-1, :-2] - padded[:, :, 1:-1, 2:]
        gradient = tension - returned + plane_weight * bending
        positions = positions - spring_rate * gradient
    return (node_flows, confidence, positions)
```

```python
import functools

import jax
import jax.numpy as jnp
import ml_dtypes
import numpy as np
from jax import lax
from jax.experimental import pallas as pl
from jax.experimental.pallas import tpu as pltpu
from jax.sharding import PartitionSpec as P

PATCH = 128
HALF = PATCH // 2
RIM = HALF // 2
STEPS = 3
SECTIONS = 4
COLS = 32
QCOLS = COLS // SECTIONS
QPIX = QCOLS * HALF
MSG = QPIX + PATCH
LANES = 128
FEATS = 16

score_scale = 800.0
spring_rate = 0.3
plane_weight = 0.5
f32 = jnp.float32
bf16 = jnp.bfloat16


def split_table(table):
    hi = table.astype(ml_dtypes.bfloat16)
    lo = (table - hi.astype(np.float64)).astype(ml_dtypes.bfloat16)
    return hi, lo


@functools.cache
def tables():
    n = np.arange(PATCH)
    angle = 2.0 * np.pi / PATCH * (np.outer(n, n) % PATCH)
    c, s = np.cos(angle), np.sin(angle)
    c[np.abs(c) < 1e-12] = 0.0
    s[np.abs(s) < 1e-12] = 0.0
    alt = (-1.0) ** n
    z = np.zeros_like(c)
    rows = np.concatenate([c[:HALF], alt[None], s[1:HALF]], axis=0)
    rows_hi, rows_lo = split_table(rows)
    rows2 = np.concatenate([rows_hi, rows_lo], axis=0)
    cols_cos = np.concatenate([c[:HALF], -s[:HALF]], axis=1)
    cols_sin = np.concatenate([-s[:HALF], -c[:HALF]], axis=1)
    even = np.concatenate([cols_cos, cols_sin], axis=0)
    odd = np.concatenate([cols_sin, cols_cos], axis=0) * np.concatenate([alt, alt])[None]
    even_hi, even_lo = split_table(even)
    odd_hi, odd_lo = split_table(odd)
    fwd = np.concatenate([even_hi, even_hi, even_lo, odd_hi, odd_hi, odd_lo], axis=0)
    inv = np.concatenate(
        [np.concatenate([c, s], axis=1), np.concatenate([-s, c], axis=1)], axis=0
    )
    inv2 = np.concatenate(split_table(inv), axis=0)
    back = np.concatenate([2.0 * c[:, :HALF], -2.0 * s[:, :HALF]], axis=1)
    back[:, 0] = 1.0
    back[:, HALF] = alt
    back_hi, back_lo = split_table(back / (PATCH * PATCH))
    back2 = np.concatenate(
        [np.concatenate([back_hi, back_hi], axis=1), np.concatenate([back_lo, back_lo], axis=1)],
        axis=0,
    )
    pair = np.concatenate([c[:HALF], -s[:HALF]], axis=1)
    zero = np.zeros_like(pair)
    edge_fwd = np.concatenate(
        [np.concatenate([pair, zero], axis=1), np.concatenate([zero, pair], axis=1)], axis=0
    )
    edge_inv = np.concatenate(
        [
            np.concatenate([c, z], axis=1),
            np.concatenate([-s, z], axis=1),
            np.concatenate([z, c], axis=1),
            np.concatenate([z, -s], axis=1),
        ],
        axis=0,
    )
    return (
        rows2,
        fwd,
        inv2,
        back2,
        np.concatenate(split_table(edge_fwd), axis=0),
        np.concatenate(split_table(edge_inv), axis=0),
    )


def dot(a, b):
    return jnp.dot(a, b, preferred_element_type=f32)


def split(x):
    hi = x.astype(bf16)
    return hi, (x - hi.astype(f32)).astype(bf16)


def dot3(x, hi, lo):
    xh, xl = split(x)
    return dot(xh, hi) + dot(xl, hi) + dot(xh, lo)


def iota(shape, dim):
    return lax.broadcasted_iota(jnp.int32, shape, dim)


def correlate_kernel(
    tile_count,
    m0, m1, m2, m3, he, ho, eq, ehe, eho, valid, off,
    rows2, fwd, inv2, back2, edge_fwd, edge_inv,
    out,
    x_ref, spec, spec0, row0, energy, u_ref, part, peak, off_s,
):
    q = lax.axis_index("sec")
    t = lax.axis_index("tile")
    even = lax.rem(t, 2) == 0
    messages = (m0, m1, m2, m3)
    at_even = pl.multiple_of(jnp.where(even, PATCH - RIM, 0), RIM)
    at_odd = pl.multiple_of(jnp.where(even, 0, PATCH - RIM), RIM)
    no_odd = jnp.logical_or(t == 0, t == tile_count - 1)
    keep = jnp.where(no_odd, 0.0, 1.0).astype(bf16)
    for i in range(2):
        x_ref[i, RIM : RIM + HALF, :] = eq[i]
        x_ref[i, pl.ds(at_even, RIM), :] = ehe[i]
        x_ref[i, pl.ds(at_odd, RIM), :] = eho[i] * keep
    for d in range(SECTIONS):
        x_ref[2 + d, RIM : RIM + HALF, :] = messages[d][...]
        x_ref[2 + d, pl.ds(at_even, RIM), :] = he[d]
        x_ref[2 + d, pl.ds(at_odd, RIM), :] = ho[d] * keep
        section = q ^ d
        off_s[section] = jnp.max(messages[d][:16, MSG - HALF :].astype(f32)).astype(jnp.int32)

    lane = iota((HALF, LANES), 1)
    low = lane < HALF
    window_row = iota((QCOLS, MSG), 0)
    window_lane = iota((QCOLS, MSG), 1)
    in_window = jnp.logical_and(
        window_lane >= window_row * HALF, window_lane < window_row * HALF + PATCH
    )
    for i in range(6):
        slot = i if i < 2 else (q ^ (i - 2)) + 2
        x = x_ref[i]
        xf = x.astype(f32)
        column = jnp.sum(xf * xf, axis=0, keepdims=True)
        windows = jnp.sum(jnp.where(in_window, column, 0.0), axis=1, keepdims=True)
        energy[slot] = jnp.broadcast_to(windows, (QCOLS, LANES))
        y2 = dot(rows2[...], x)
        y = y2[:PATCH] + y2[PATCH:]
        evens, odds = [], []
        for v in range(QCOLS // 2 + 1):
            a = y[:HALF, LANES * v : LANES * (v + 1)]
            b = pltpu.roll(y[HALF:, LANES * v : LANES * (v + 1)], HALF, 1)
            g = jnp.where(low, a, b)
            evens.append(g)
            row0[16 * i + 2 * v : 16 * i + 2 * v + 1, :] = g[0:1]
            if v < QCOLS // 2:
                g = jnp.where(low, b, a)
                odds.append(g)
                row0[16 * i + 2 * v + 1 : 16 * i + 2 * v + 2, :] = pltpu.roll(g[0:1], HALF, 1)
        row0[16 * i + QCOLS + 1 : 16 * i + 16, :] = jnp.zeros((7, LANES), f32)
        gh, gl = split(jnp.concatenate(evens, axis=0))
        de = dot(jnp.concatenate([gh, gl], axis=1), fwd[0:256]) + dot(gh, fwd[256:384])
        gh, gl = split(jnp.concatenate(odds, axis=0))
        do = dot(jnp.concatenate([gh, gl], axis=1), fwd[384:640]) + dot(gh, fwd[640:768])
        for j in range(QCOLS):
            v = j // 2
            if j % 2 == 0:
                first, second = de[HALF * v : HALF * (v + 1)], do[HALF * v : HALF * (v + 1)]
            else:
                first, second = do[HALF * v : HALF * (v + 1)], de[HALF * (v + 1) : HALF * (v + 2)]
            spec[slot, j] = first + second

    d0 = dot3(row0[...], edge_fwd[0:PATCH], edge_fwd[PATCH:])
    flip = (iota(d0.shape, 0) & iota(d0.shape, 1) & 1) == 1
    d0 = jnp.where(flip, -d0, d0)
    for i in range(6):
        slot = i if i < 2 else (q ^ (i - 2)) + 2
        spec0[slot] = d0[16 * i : 16 * i + QCOLS] + d0[16 * i + 1 : 16 * i + QCOLS + 1]
    products = []
    prior = []
    for s in range(SECTIONS):
        prev = s + 2 - off_s[s]
        prior.append(prev)
        f, g = spec0[s + 2], spec0[prev]
        parts = []
        for h in range(2):
            fr, fi = f[:, 256 * h : 256 * h + 128], f[:, 256 * h + 128 : 256 * h + 256]
            gr, gi = g[:, 256 * h : 256 * h + 128], g[:, 256 * h + 128 : 256 * h + 256]
            parts += [fr * gr + fi * gi, fi * gr - fr * gi]
        products.append(jnp.concatenate(parts, axis=1))
    u0 = dot3(jnp.concatenate(products, axis=0), edge_inv[0:512], edge_inv[512:])

    lane1 = iota((1, LANES), 1)
    shift_lane = jnp.where(lane1 < HALF, lane1, lane1 - PATCH).astype(f32)
    sub8 = iota((8, LANES), 0).astype(f32)
    scales = []
    for s in range(SECTIONS):
        prev = prior[s]
        scale8 = score_scale / jnp.sqrt(energy[s + 2] * energy[prev] + 1e-6)
        scales.append(scale8)
        highs, lows = [], []
        for j in range(QCOLS):
            f, g = spec[s + 2, j], spec[prev, j]
            fr, fi = f[:, :PATCH], f[:, PATCH:]
            gr, gi = g[:, :PATCH], g[:, PATCH:]
            ph, plo = split(jnp.concatenate([fr * gr + fi * gi, fi * gr - fr * gi], axis=1))
            highs.append(ph)
            lows.append(plo)
        ph, plo = jnp.concatenate(highs, axis=0), jnp.concatenate(lows, axis=0)
        u = dot(ph, inv2[0:256]) + dot(plo, inv2[0:256]) + dot(ph, inv2[256:512])
        for j in range(QCOLS):
            u_ref[s, j] = u[HALF * j : HALF * (j + 1)]
            u_ref[s, j, 0:1, :] = u0[QCOLS * s + j : QCOLS * s + j + 1]
        for j in range(0, QCOLS, 2):
            sides = []
            for k in (j, j + 1):
                uh, ul = split(u_ref[s, k])
                sides.append(
                    jnp.concatenate([uh[:, :PATCH], uh[:, PATCH:], ul[:, :PATCH], ul[:, PATCH:]], axis=0)
                )
            c2 = dot(back2[...], jnp.concatenate(sides, axis=1))
            both = c2[:PATCH] + c2[PATCH:]
            for k in (j, j + 1):
                c = both[:, PATCH * (k - j) : PATCH * (k - j + 1)]
                top = jnp.max(jnp.max(c, axis=0, keepdims=True), axis=1, keepdims=True)
                rate = scale8[k : k + 1, :]
                w = jnp.exp((c - top) * rate)
                total = w[0:8]
                moment = jnp.zeros((8, LANES), f32)
                for a in range(1, PATCH // 8):
                    block = w[8 * a : 8 * a + 8]
                    total = total + block
                    moment = moment + block * float(8 * a if 8 * a < HALF else 8 * a - PATCH)
                moment = moment + total * sub8
                total = jnp.sum(total, axis=0, keepdims=True)
                part[k, s : s + 1, :] = jnp.sum(moment, axis=0, keepdims=True)
                part[k, 4 + s : 5 + s, :] = total * shift_lane
                part[k, 8 + s : 9 + s, :] = total
                peak[k, s : s + 1, :] = jnp.broadcast_to(top, (1, LANES))

    lane16 = iota((FEATS, LANES), 1)
    lane4 = iota((SECTIONS, LANES), 1)
    lane8 = iota((QCOLS, LANES), 1)
    first_lane = q * QCOLS
    sums = jnp.zeros((FEATS, LANES), f32)
    tops = jnp.zeros((SECTIONS, LANES), f32)
    for j in range(QCOLS):
        part[j, 12:16, :] = jnp.zeros((4, LANES), f32)
        sums = sums + jnp.where(
            lane16 == first_lane + j, jnp.sum(part[j], axis=1, keepdims=True), 0.0
        )
        tops = tops + jnp.where(lane4 == first_lane + j, peak[j], 0.0)
    pick = lane8 == first_lane + iota((QCOLS, LANES), 0)
    rates = jnp.concatenate(
        [jnp.sum(jnp.where(pick, scale8, 0.0), axis=0, keepdims=True) for scale8 in scales], axis=0
    )
    mine = jnp.logical_and(lane4 >= first_lane, lane4 < first_lane + QCOLS)
    total = jnp.where(mine, sums[8:12], 1.0)
    out[0:4, :] = sums[0:4] / total
    out[4:8, :] = sums[4:8] / total
    out[8:12, :] = jnp.where(mine, (tops * rates + jnp.log(total)) / score_scale, 0.0)
    row4 = iota((SECTIONS, LANES), 0)
    flags = jnp.concatenate(
        [valid[0].astype(f32), jnp.broadcast_to(off[...], (1, COLS)), jnp.zeros((1, HALF), f32)],
        axis=1,
    )
    out[12:16, :] = jnp.where(row4 == q, flags, 0.0)


def relax_kernel(tile_count, own, near, far, third, flows_out, conf_out, pos_out):
    q = lax.axis_index("sec")
    t = lax.axis_index("tile")
    even = lax.rem(t, 2) == 0
    step = jnp.where(even, 1, -1)
    inside = lambda row: jnp.logical_and(row >= 0, row < tile_count)
    rows = [far[1], far[0], own[...], near[...], third[...]]
    shape = (2 * SECTIONS, LANES)
    lane = iota(shape, 1)
    row = iota(shape, 0)
    sec = lax.rem(row, SECTIONS)
    live = lane < COLS
    offsets = jnp.max(
        jnp.where(iota((SECTIONS, LANES), 1) >= COLS, own[12:16, :], 0.0), axis=1, keepdims=True
    )
    offsets = jnp.broadcast_to(jnp.concatenate([offsets, offsets], axis=0), shape)
    one = offsets < 1.5
    flows, stiff, present = [], [], []
    for i, cells in enumerate(rows):
        ok = jnp.logical_and(live, inside(t + step * (i - 2)))
        present.append(ok)
        flows.append(jnp.where(ok, cells[0:8], 0.0))
        stiffness = cells[8:12] * cells[12:16]
        stiff.append(jnp.where(ok, jnp.concatenate([stiffness, stiffness], axis=0), 0.0))

    def back(x, n):
        return jnp.where(sec >= n, pltpu.roll(x, n, 0), 0.0)

    def ahead(x, n):
        return jnp.where(sec < SECTIONS - n, pltpu.roll(x, 2 * SECTIONS - n, 0), 0.0)

    zero = jnp.zeros(shape, f32)
    positions = [zero] * 5
    for iteration in range(STEPS):
        new = list(positions)
        for i in range(iteration, 5 - iteration):
            p = positions[i]
            if iteration == 0:
                tension = stiff[i] * flows[i]
                bending = zero
            else:
                pulled = jnp.where(one, back(p, 1), back(p, 2))
                tension = stiff[i] * (p - pulled + flows[i])
                bending = (
                    4.0 * p
                    - positions[i - 1]
                    - positions[i + 1]
                    - pltpu.roll(p, 1, 1)
                    - pltpu.roll(p, LANES - 1, 1)
                )
            returned = ahead(jnp.where(one, tension, 0.0), 1) + ahead(jnp.where(one, 0.0, tension), 2)
            gradient = tension - returned + plane_weight * bending
            new[i] = jnp.where(present[i], p - spring_rate * gradient, 0.0)
        positions = new
    for c in range(2):
        chosen = row == q + SECTIONS * c
        flows_out[0, c] = jnp.sum(jnp.where(chosen, flows[2], 0.0), axis=0, keepdims=True)[:, :COLS]
        pos_out[0, c] = jnp.sum(jnp.where(chosen, positions[2], 0.0), axis=0, keepdims=True)[:, :COLS]
    chosen = iota((SECTIONS, LANES), 0) == q
    conf_out[0] = jnp.sum(jnp.where(chosen, own[8:12, :], 0.0), axis=0, keepdims=True)[:, :COLS]


def xor_route(count, d):
    return [(i, i ^ d) for i in range(count)]


def odd_route(count):
    return [(i, min(max(i + (1 if i % 2 else -1), 0), count - 1)) for i in range(count)]


def per_device(sections, earlier, offsets, patch_valid):
    tile_count = lax.axis_size("tile")
    q = lax.axis_index("sec")
    t = lax.axis_index("tile")
    even = t % 2 == 0
    swap_even = functools.partial(lax.ppermute, axis_name="tile", perm=xor_route(tile_count, 1))
    swap_odd = functools.partial(lax.ppermute, axis_name="tile", perm=odd_route(tile_count))
    width = 2 * RIM + COLS * HALF + HALF
    offset = offsets.astype(bf16)
    wide = jnp.pad(sections[0], ((0, 0), (RIM, width - RIM - COLS * HALF)))
    marked = lax.broadcasted_iota(jnp.int32, (HALF, MSG), 1) >= MSG - HALF

    def message(d):
        cut = lax.dynamic_slice_in_dim(wide, QPIX * (q ^ d), MSG, axis=1)
        return jnp.where(marked, offset[0], cut)

    messages = [message(d) for d in range(SECTIONS)]
    got = [messages[0]]
    for d in (2, 3, 1):
        got.append(lax.ppermute(messages[d], "sec", xor_route(SECTIONS, d)))
    got = [got[0], got[3], got[1], got[2]]
    eq = lax.dynamic_slice_in_dim(
        jnp.pad(earlier, ((0, 0), (0, 0), (RIM, width - RIM - COLS * HALF))), QPIX * q, MSG, axis=2
    )
    to_even = jnp.where(even, RIM, 0)
    to_odd = jnp.where(even, 0, RIM)
    e_even = swap_even(lax.dynamic_slice_in_dim(eq, to_even, RIM, axis=1))
    e_odd = swap_odd(lax.dynamic_slice_in_dim(eq, to_odd, RIM, axis=1))
    stacked = jnp.stack(got)
    h_odd = swap_odd(lax.dynamic_slice_in_dim(stacked, to_odd, RIM, axis=1))
    h_even = swap_even(lax.dynamic_slice_in_dim(stacked, to_even, RIM, axis=1))
    vmem = pl.BlockSpec(memory_space=pltpu.VMEM)
    consts = [jnp.asarray(x) for x in tables()]
    cells = pl.pallas_call(
        functools.partial(correlate_kernel, tile_count),
        out_shape=jax.ShapeDtypeStruct((FEATS, LANES), f32),
        in_specs=[vmem] * 17,
        out_specs=vmem,
        scratch_shapes=[
            pltpu.VMEM((6, PATCH, MSG), bf16),
            pltpu.VMEM((6, QCOLS, HALF, 256), f32),
            pltpu.VMEM((6, QCOLS, 512), f32),
            pltpu.VMEM((96, LANES), f32),
            pltpu.VMEM((6, QCOLS, LANES), f32),
            pltpu.VMEM((SECTIONS, QCOLS, HALF, 256), f32),
            pltpu.VMEM((QCOLS, FEATS, LANES), f32),
            pltpu.VMEM((QCOLS, SECTIONS, LANES), f32),
            pltpu.SMEM((SECTIONS,), jnp.int32),
        ],
        compiler_params=pltpu.CompilerParams(vmem_limit_bytes=48 * 1024 * 1024),
        name="correlate",
    )(*got, h_even, h_odd, eq, e_even, e_odd, patch_valid, offsets.astype(f32)[None], *consts)
    cells = cells + lax.ppermute(cells, "sec", xor_route(SECTIONS, 1))
    cells = cells + lax.ppermute(cells, "sec", xor_route(SECTIONS, 2))
    near = swap_even(cells)
    far = swap_odd(jnp.stack([cells, near]))
    third = swap_even(far[0])
    return pl.pallas_call(
        functools.partial(relax_kernel, tile_count),
        out_shape=(
            jax.ShapeDtypeStruct((1, 2, 1, COLS), f32),
            jax.ShapeDtypeStruct((1, 1, COLS), f32),
            jax.ShapeDtypeStruct((1, 2, 1, COLS), f32),
        ),
        in_specs=[vmem] * 4,
        out_specs=(vmem,) * 3,
        name="relax",
    )(cells, near, far, third)


def solution(mesh):
    in_specs = (P("sec", "tile", None), P(None, "tile", None), P("sec"), P("sec", "tile", None))
    out_specs = (P("sec", None, "tile", None), P("sec", "tile", None), P("sec", None, "tile", None))
    return jax.shard_map(
        per_device, mesh=mesh, in_specs=in_specs, out_specs=out_specs, check_vma=False
    )
```

```python
import functools

import jax
import jax.numpy as jnp
import ml_dtypes
import numpy as np
from jax import lax
from jax.experimental import pallas as pl
from jax.experimental.pallas import tpu as pltpu
from jax.sharding import PartitionSpec as P

PATCH = 128
HALF = PATCH // 2
RIM = HALF // 2
STEPS = 3
SECTIONS = 4
COLS = 32
QCOLS = COLS // SECTIONS
QPIX = QCOLS * HALF
MSG = QPIX + PATCH
HALF_MSG = 2 * QPIX + PATCH
LANES = 128
FEATS = 16

score_scale = 800.0
spring_rate = 0.3
plane_weight = 0.5
f32 = jnp.float32
bf16 = jnp.bfloat16


def split_table(table):
    hi = table.astype(ml_dtypes.bfloat16)
    lo = (table - hi.astype(np.float64)).astype(ml_dtypes.bfloat16)
    return hi, lo


@functools.cache
def tables():
    n = np.arange(PATCH)
    angle = 2.0 * np.pi / PATCH * (np.outer(n, n) % PATCH)
    c, s = np.cos(angle), np.sin(angle)
    c[np.abs(c) < 1e-12] = 0.0
    s[np.abs(s) < 1e-12] = 0.0
    alt = (-1.0) ** n
    z = np.zeros_like(c)
    rows = np.concatenate([c[:HALF], alt[None], s[1:HALF]], axis=0)
    rows_hi, rows_lo = split_table(rows)
    rows2 = np.concatenate([rows_hi, rows_lo], axis=0)
    cols_cos = np.concatenate([c[:HALF], -s[:HALF]], axis=1)
    cols_sin = np.concatenate([-s[:HALF], -c[:HALF]], axis=1)
    even = np.concatenate([cols_cos, cols_sin], axis=0)
    odd = np.concatenate([cols_sin, cols_cos], axis=0) * np.concatenate([alt, alt])[None]
    even_hi, even_lo = split_table(even)
    odd_hi, odd_lo = split_table(odd)
    fwd = np.concatenate([even_hi, even_hi, even_lo, odd_hi, odd_hi, odd_lo], axis=0)
    inv = np.concatenate(
        [np.concatenate([c, s], axis=1), np.concatenate([-s, c], axis=1)], axis=0
    )
    inv2 = np.concatenate(split_table(inv), axis=0)
    back = np.concatenate([2.0 * c[:, :HALF], -2.0 * s[:, :HALF]], axis=1)
    back[:, 0] = 1.0
    back[:, HALF] = alt
    back_hi, back_lo = split_table(back / (PATCH * PATCH))
    back2 = np.concatenate(
        [np.concatenate([back_hi, back_hi], axis=1), np.concatenate([back_lo, back_lo], axis=1)],
        axis=0,
    )
    pair = np.concatenate([c[:HALF], -s[:HALF]], axis=1)
    zero = np.zeros_like(pair)
    edge_fwd = np.concatenate(
        [np.concatenate([pair, zero], axis=1), np.concatenate([zero, pair], axis=1)], axis=0
    )
    edge_inv = np.concatenate(
        [
            np.concatenate([c, z], axis=1),
            np.concatenate([-s, z], axis=1),
            np.concatenate([z, c], axis=1),
            np.concatenate([z, -s], axis=1),
        ],
        axis=0,
    )
    return (
        rows2,
        fwd,
        inv2,
        back2,
        np.concatenate(split_table(edge_fwd), axis=0),
        np.concatenate(split_table(edge_inv), axis=0),
    )


def dot(a, b):
    return jnp.dot(a, b, preferred_element_type=f32)


def split(x):
    hi = x.astype(bf16)
    return hi, (x - hi.astype(f32)).astype(bf16)


def dot3(x, hi, lo):
    xh, xl = split(x)
    return dot(xh, hi) + dot(xl, hi) + dot(xh, lo)


def iota(shape, dim):
    return lax.broadcasted_iota(jnp.int32, shape, dim)


def correlate_kernel(
    tile_count,
    mine, sib, eq, near, far, valid, off,
    rows2, fwd, inv2, back2, edge_fwd, edge_inv,
    out,
    x_ref, spec, spec0, row0, energy, u_ref, part, peak, off_s,
):
    q = lax.axis_index("sec")
    t = lax.axis_index("tile")
    even = lax.rem(t, 2) == 0
    at_even = pl.multiple_of(jnp.where(even, PATCH - RIM, 0), RIM)
    at_odd = pl.multiple_of(jnp.where(even, 0, PATCH - RIM), RIM)
    no_odd = jnp.logical_or(t == 0, t == tile_count - 1)
    keep = jnp.where(no_odd, 0.0, 1.0).astype(bf16)
    centers = [eq.at[0], eq.at[1], mine.at[0], mine.at[1], sib.at[0], sib.at[1]]
    slots = [0, 1, q + 2, (q ^ 2) + 2, (q ^ 1) + 2, (q ^ 3) + 2]
    for i, center in enumerate(centers):
        x_ref[i, RIM : RIM + HALF, :] = center[...]
        x_ref[i, pl.ds(at_even, RIM), :] = near[i]
        x_ref[i, pl.ds(at_odd, RIM), :] = far[i] * keep
        if i >= 2:
            offset = jnp.max(center[:16, MSG - HALF :].astype(f32))
            off_s[slots[i] - 2] = offset.astype(jnp.int32)

    lane = iota((HALF, LANES), 1)
    low = lane < HALF
    window_row = iota((QCOLS, MSG), 0)
    window_lane = iota((QCOLS, MSG), 1)
    in_window = jnp.logical_and(
        window_lane >= window_row * HALF, window_lane < window_row * HALF + PATCH
    )
    for i in range(6):
        slot = slots[i]
        x = x_ref[i]
        xf = x.astype(f32)
        column = jnp.sum(xf * xf, axis=0, keepdims=True)
        windows = jnp.sum(jnp.where(in_window, column, 0.0), axis=1, keepdims=True)
        energy[slot] = jnp.broadcast_to(windows, (QCOLS, LANES))
        y2 = dot(rows2[...], x)
        y = y2[:PATCH] + y2[PATCH:]
        evens, odds = [], []
        for v in range(QCOLS // 2 + 1):
            a = y[:HALF, LANES * v : LANES * (v + 1)]
            b = pltpu.roll(y[HALF:, LANES * v : LANES * (v + 1)], HALF, 1)
            g = jnp.where(low, a, b)
            evens.append(g)
            row0[16 * i + 2 * v : 16 * i + 2 * v + 1, :] = g[0:1]
            if v < QCOLS // 2:
                g = jnp.where(low, b, a)
                odds.append(g)
                row0[16 * i + 2 * v + 1 : 16 * i + 2 * v + 2, :] = pltpu.roll(g[0:1], HALF, 1)
        row0[16 * i + QCOLS + 1 : 16 * i + 16, :] = jnp.zeros((7, LANES), f32)
        gh, gl = split(jnp.concatenate(evens, axis=0))
        de = dot(jnp.concatenate([gh, gl], axis=1), fwd[0:256]) + dot(gh, fwd[256:384])
        gh, gl = split(jnp.concatenate(odds, axis=0))
        do = dot(jnp.concatenate([gh, gl], axis=1), fwd[384:640]) + dot(gh, fwd[640:768])
        for j in range(QCOLS):
            v = j // 2
            if j % 2 == 0:
                first, second = de[HALF * v : HALF * (v + 1)], do[HALF * v : HALF * (v + 1)]
            else:
                first, second = do[HALF * v : HALF * (v + 1)], de[HALF * (v + 1) : HALF * (v + 2)]
            spec[slot, j] = first + second

    d0 = dot3(row0[...], edge_fwd[0:PATCH], edge_fwd[PATCH:])
    flip = (iota(d0.shape, 0) & iota(d0.shape, 1) & 1) == 1
    d0 = jnp.where(flip, -d0, d0)
    for i in range(6):
        slot = slots[i]
        spec0[slot] = d0[16 * i : 16 * i + QCOLS] + d0[16 * i + 1 : 16 * i + QCOLS + 1]
    products = []
    prior = []
    for s in range(SECTIONS):
        prev = s + 2 - off_s[s]
        prior.append(prev)
        f, g = spec0[s + 2], spec0[prev]
        parts = []
        for h in range(2):
            fr, fi = f[:, 256 * h : 256 * h + 128], f[:, 256 * h + 128 : 256 * h + 256]
            gr, gi = g[:, 256 * h : 256 * h + 128], g[:, 256 * h + 128 : 256 * h + 256]
            parts += [fr * gr + fi * gi, fi * gr - fr * gi]
        products.append(jnp.concatenate(parts, axis=1))
    u0 = dot3(jnp.concatenate(products, axis=0), edge_inv[0:512], edge_inv[512:])

    lane1 = iota((1, LANES), 1)
    shift_lane = jnp.where(lane1 < HALF, lane1, lane1 - PATCH).astype(f32)
    sub8 = iota((8, LANES), 0).astype(f32)
    scales = []
    for s in range(SECTIONS):
        prev = prior[s]
        scale8 = score_scale / jnp.sqrt(energy[s + 2] * energy[prev] + 1e-6)
        scales.append(scale8)
        highs, lows = [], []
        for j in range(QCOLS):
            f, g = spec[s + 2, j], spec[prev, j]
            fr, fi = f[:, :PATCH], f[:, PATCH:]
            gr, gi = g[:, :PATCH], g[:, PATCH:]
            ph, plo = split(jnp.concatenate([fr * gr + fi * gi, fi * gr - fr * gi], axis=1))
            highs.append(ph)
            lows.append(plo)
        ph, plo = jnp.concatenate(highs, axis=0), jnp.concatenate(lows, axis=0)
        u = dot(ph, inv2[0:256]) + dot(plo, inv2[0:256]) + dot(ph, inv2[256:512])
        for j in range(QCOLS):
            u_ref[s, j] = u[HALF * j : HALF * (j + 1)]
            u_ref[s, j, 0:1, :] = u0[QCOLS * s + j : QCOLS * s + j + 1]
        for j in range(0, QCOLS, 2):
            sides = []
            for k in (j, j + 1):
                uh, ul = split(u_ref[s, k])
                sides.append(
                    jnp.concatenate([uh[:, :PATCH], uh[:, PATCH:], ul[:, :PATCH], ul[:, PATCH:]], axis=0)
                )
            c2 = dot(back2[...], jnp.concatenate(sides, axis=1))
            both = c2[:PATCH] + c2[PATCH:]
            for k in (j, j + 1):
                c = both[:, PATCH * (k - j) : PATCH * (k - j + 1)]
                top = jnp.max(jnp.max(c, axis=0, keepdims=True), axis=1, keepdims=True)
                rate = scale8[k : k + 1, :]
                w = jnp.exp((c - top) * rate)
                total = w[0:8]
                moment = jnp.zeros((8, LANES), f32)
                for a in range(1, PATCH // 8):
                    block = w[8 * a : 8 * a + 8]
                    total = total + block
                    moment = moment + block * float(8 * a if 8 * a < HALF else 8 * a - PATCH)
                moment = moment + total * sub8
                total = jnp.sum(total, axis=0, keepdims=True)
                part[k, s : s + 1, :] = jnp.sum(moment, axis=0, keepdims=True)
                part[k, 4 + s : 5 + s, :] = total * shift_lane
                part[k, 8 + s : 9 + s, :] = total
                peak[k, s : s + 1, :] = jnp.broadcast_to(top, (1, LANES))

    lane16 = iota((FEATS, LANES), 1)
    lane4 = iota((SECTIONS, LANES), 1)
    lane8 = iota((QCOLS, LANES), 1)
    first_lane = q * QCOLS
    sums = jnp.zeros((FEATS, LANES), f32)
    tops = jnp.zeros((SECTIONS, LANES), f32)
    for j in range(QCOLS):
        part[j, 12:16, :] = jnp.zeros((4, LANES), f32)
        sums = sums + jnp.where(
            lane16 == first_lane + j, jnp.sum(part[j], axis=1, keepdims=True), 0.0
        )
        tops = tops + jnp.where(lane4 == first_lane + j, peak[j], 0.0)
    pick = lane8 == first_lane + iota((QCOLS, LANES), 0)
    rates = jnp.concatenate(
        [jnp.sum(jnp.where(pick, scale8, 0.0), axis=0, keepdims=True) for scale8 in scales], axis=0
    )
    mine = jnp.logical_and(lane4 >= first_lane, lane4 < first_lane + QCOLS)
    total = jnp.where(mine, sums[8:12], 1.0)
    out[0:4, :] = sums[0:4] / total
    out[4:8, :] = sums[4:8] / total
    out[8:12, :] = jnp.where(mine, (tops * rates + jnp.log(total)) / score_scale, 0.0)
    row4 = iota((SECTIONS, LANES), 0)
    flags = jnp.concatenate(
        [valid[0].astype(f32), jnp.broadcast_to(off[...], (1, COLS)), jnp.zeros((1, HALF), f32)],
        axis=1,
    )
    out[12:16, :] = jnp.where(row4 == q, flags, 0.0)


def relax_kernel(tile_count, own, near, far, third, flows_out, conf_out, pos_out):
    q = lax.axis_index("sec")
    t = lax.axis_index("tile")
    even = lax.rem(t, 2) == 0
    step = jnp.where(even, 1, -1)
    inside = lambda row: jnp.logical_and(row >= 0, row < tile_count)
    rows = [far[1], far[0], own[...], near[...], third[...]]
    shape = (2 * SECTIONS, LANES)
    lane = iota(shape, 1)
    row = iota(shape, 0)
    sec = lax.rem(row, SECTIONS)
    live = lane < COLS
    offsets = jnp.max(
        jnp.where(iota((SECTIONS, LANES), 1) >= COLS, own[12:16, :], 0.0), axis=1, keepdims=True
    )
    offsets = jnp.broadcast_to(jnp.concatenate([offsets, offsets], axis=0), shape)
    one = offsets < 1.5
    flows, stiff, present = [], [], []
    for i, cells in enumerate(rows):
        ok = jnp.logical_and(live, inside(t + step * (i - 2)))
        present.append(ok)
        flows.append(jnp.where(ok, cells[0:8], 0.0))
        stiffness = cells[8:12] * cells[12:16]
        stiff.append(jnp.where(ok, jnp.concatenate([stiffness, stiffness], axis=0), 0.0))

    def back(x, n):
        return jnp.where(sec >= n, pltpu.roll(x, n, 0), 0.0)

    def ahead(x, n):
        return jnp.where(sec < SECTIONS - n, pltpu.roll(x, 2 * SECTIONS - n, 0), 0.0)

    zero = jnp.zeros(shape, f32)
    positions = [zero] * 5
    for iteration in range(STEPS):
        new = list(positions)
        for i in range(iteration, 5 - iteration):
            p = positions[i]
            if iteration == 0:
                tension = stiff[i] * flows[i]
                bending = zero
            else:
                pulled = jnp.where(one, back(p, 1), back(p, 2))
                tension = stiff[i] * (p - pulled + flows[i])
                bending = (
                    4.0 * p
                    - positions[i - 1]
                    - positions[i + 1]
                    - pltpu.roll(p, 1, 1)
                    - pltpu.roll(p, LANES - 1, 1)
                )
            returned = ahead(jnp.where(one, tension, 0.0), 1) + ahead(jnp.where(one, 0.0, tension), 2)
            gradient = tension - returned + plane_weight * bending
            new[i] = jnp.where(present[i], p - spring_rate * gradient, 0.0)
        positions = new
    for c in range(2):
        chosen = row == q + SECTIONS * c
        flows_out[0, c] = jnp.sum(jnp.where(chosen, flows[2], 0.0), axis=0, keepdims=True)[:, :COLS]
        pos_out[0, c] = jnp.sum(jnp.where(chosen, positions[2], 0.0), axis=0, keepdims=True)[:, :COLS]
    chosen = iota((SECTIONS, LANES), 0) == q
    conf_out[0] = jnp.sum(jnp.where(chosen, own[8:12, :], 0.0), axis=0, keepdims=True)[:, :COLS]


def xor_route(count, d):
    return [(i, i ^ d) for i in range(count)]


def joint_route(tile_count, odd):
    route = []
    for s in range(SECTIONS):
        for t in range(tile_count):
            to = t ^ 1 if not odd else t + (1 if t % 2 else -1)
            pair = (s, to) if 0 <= to < tile_count else (s ^ 1, t)
            route.append((s * tile_count + t, pair[0] * tile_count + pair[1]))
    return route


def per_device(sections, earlier, offsets, patch_valid):
    tile_count = lax.axis_size("tile")
    q = lax.axis_index("sec")
    t = lax.axis_index("tile")
    even = t % 2 == 0
    swap = functools.partial(lax.ppermute, axis_name=("sec", "tile"))
    swap_even = functools.partial(swap, perm=joint_route(tile_count, False))
    swap_odd = functools.partial(swap, perm=joint_route(tile_count, True))
    right = 2 * QPIX * (SECTIONS // 2 - 1) + HALF_MSG - RIM - COLS * HALF
    offset = offsets.astype(bf16)[0]
    wide = jnp.pad(sections[0], ((0, 0), (RIM, right)))
    half_lane = lax.broadcasted_iota(jnp.int32, (HALF, HALF_MSG), 1)

    def half(h):
        cut = lax.dynamic_slice_in_dim(wide, 2 * QPIX * h, HALF_MSG, axis=1)
        return jnp.where(half_lane >= HALF_MSG - HALF, offset, cut)

    own = half(q // 2)
    across = lax.ppermute(half(1 - q // 2), "sec", xor_route(SECTIONS, 2))

    def quarter(strip, c):
        cut = lax.dynamic_slice_in_dim(strip, QPIX * c, MSG - HALF, axis=1)
        return jnp.concatenate([cut, strip[:, HALF_MSG - HALF :]], axis=1)

    def quarters(c):
        return jnp.stack([quarter(own, c), quarter(across, c)])

    core = q % 2
    mine = quarters(core)
    sib = lax.ppermute(quarters(1 - core), "sec", xor_route(SECTIONS, 1))
    eq = lax.dynamic_slice_in_dim(
        jnp.pad(earlier, ((0, 0), (0, 0), (RIM, right))), QPIX * q, MSG, axis=2
    )
    to_even = jnp.where(even, RIM, 0)
    to_odd = jnp.where(even, 0, RIM)

    def rows(start):
        return jnp.concatenate(
            [lax.dynamic_slice_in_dim(x, start, RIM, axis=1) for x in (eq, mine, sib)], axis=0
        )

    far = swap_odd(rows(to_odd))
    near = swap_even(rows(to_even))
    vmem = pl.BlockSpec(memory_space=pltpu.VMEM)
    consts = [jnp.asarray(x) for x in tables()]
    cells = pl.pallas_call(
        functools.partial(correlate_kernel, tile_count),
        out_shape=jax.ShapeDtypeStruct((FEATS, LANES), f32),
        in_specs=[vmem] * 13,
        out_specs=vmem,
        scratch_shapes=[
            pltpu.VMEM((6, PATCH, MSG), bf16),
            pltpu.VMEM((6, QCOLS, HALF, 256), f32),
            pltpu.VMEM((6, QCOLS, 512), f32),
            pltpu.VMEM((96, LANES), f32),
            pltpu.VMEM((6, QCOLS, LANES), f32),
            pltpu.VMEM((SECTIONS, QCOLS, HALF, 256), f32),
            pltpu.VMEM((QCOLS, FEATS, LANES), f32),
            pltpu.VMEM((QCOLS, SECTIONS, LANES), f32),
            pltpu.SMEM((SECTIONS,), jnp.int32),
        ],
        compiler_params=pltpu.CompilerParams(vmem_limit_bytes=48 * 1024 * 1024),
        name="correlate",
    )(mine, sib, eq, near, far, patch_valid, offsets.astype(f32)[None], *consts)
    cells = cells + lax.ppermute(cells, "sec", xor_route(SECTIONS, 1))
    cells = cells + lax.ppermute(cells, "sec", xor_route(SECTIONS, 2))
    near = swap_even(cells)
    far = swap_odd(jnp.stack([cells, near]))
    third = swap_even(far[0])
    return pl.pallas_call(
        functools.partial(relax_kernel, tile_count),
        out_shape=(
            jax.ShapeDtypeStruct((1, 2, 1, COLS), f32),
            jax.ShapeDtypeStruct((1, 1, COLS), f32),
            jax.ShapeDtypeStruct((1, 2, 1, COLS), f32),
        ),
        in_specs=[vmem] * 4,
        out_specs=(vmem,) * 3,
        compiler_params=pltpu.CompilerParams(vmem_limit_bytes=8 * 1024 * 1024),
        name="relax",
    )(cells, near, far, third)


def solution(mesh):
    in_specs = (P("sec", "tile", None), P(None, "tile", None), P("sec"), P("sec", "tile", None))
    out_specs = (P("sec", None, "tile", None), P("sec", "tile", None), P("sec", None, "tile", None))
    return jax.shard_map(
        per_device, mesh=mesh, in_specs=in_specs, out_specs=out_specs, check_vma=False
    )
```

```python
import functools

import jax
import jax.numpy as jnp
import ml_dtypes
import numpy as np
from jax import lax
from jax.experimental import pallas as pl
from jax.experimental.pallas import tpu as pltpu
from jax.sharding import PartitionSpec as P

PATCH = 128
HALF = PATCH // 2
RIM = HALF // 2
STEPS = 3
SECTIONS = 4
COLS = 32
QCOLS = COLS // SECTIONS
QPIX = QCOLS * HALF
MSG = QPIX + PATCH
HALF_MSG = 2 * QPIX + PATCH
LANES = 128
FEATS = 16

score_scale = 800.0
spring_rate = 0.3
plane_weight = 0.5
f32 = jnp.float32
bf16 = jnp.bfloat16


def split_table(table):
    hi = table.astype(ml_dtypes.bfloat16)
    lo = (table - hi.astype(np.float64)).astype(ml_dtypes.bfloat16)
    return hi, lo


@functools.cache
def tables():
    n = np.arange(PATCH)
    angle = 2.0 * np.pi / PATCH * (np.outer(n, n) % PATCH)
    c, s = np.cos(angle), np.sin(angle)
    c[np.abs(c) < 1e-12] = 0.0
    s[np.abs(s) < 1e-12] = 0.0
    alt = (-1.0) ** n
    rows = np.concatenate([c[:HALF], alt[None], s[1:HALF]], axis=0)
    rows_hi, rows_lo = split_table(rows)
    rows2 = np.concatenate([rows_hi, rows_lo], axis=0)
    cols_cos = np.concatenate([c[:HALF], -s[:HALF]], axis=1)
    cols_sin = np.concatenate([-s[:HALF], -c[:HALF]], axis=1)
    even = np.concatenate([cols_cos, cols_sin], axis=0)
    odd = np.concatenate([cols_sin, cols_cos], axis=0) * np.concatenate([alt, alt])[None]
    even_hi, even_lo = split_table(even)
    odd_hi, odd_lo = split_table(odd)
    fwd = np.concatenate([even_hi, even_hi, even_lo, odd_hi, odd_hi, odd_lo], axis=0)
    inv = np.concatenate(
        [np.concatenate([c, s], axis=1), np.concatenate([-s, c], axis=1)], axis=0
    )
    inv2 = np.concatenate(split_table(inv), axis=0)
    back = np.concatenate([2.0 * c[:, :HALF], -2.0 * s[:, :HALF]], axis=1)
    back[:, 0] = 1.0
    back[:, HALF] = alt
    back_hi, back_lo = split_table(back / (PATCH * PATCH))
    back2 = np.concatenate(
        [np.concatenate([back_hi, back_hi], axis=1), np.concatenate([back_lo, back_lo], axis=1)],
        axis=0,
    )
    return (
        rows2,
        fwd,
        inv2,
        back2,
    )


def dot(a, b):
    return jnp.dot(a, b, preferred_element_type=f32)


def split(x):
    hi = x.astype(bf16)
    return hi, (x - hi.astype(f32)).astype(bf16)


def dot3(x, hi, lo):
    xh, xl = split(x)
    return dot(xh, hi) + dot(xl, hi) + dot(xh, lo)


def iota(shape, dim):
    return lax.broadcasted_iota(jnp.int32, shape, dim)


def correlate_kernel(
    tile_count,
    mine, sib, eq, near, far, valid, off,
    rows2, fwd, inv2, back2,
    out,
    x_ref, spec, spec0, row0, energy, u_ref, part, peak, off_s,
):
    q = lax.axis_index("sec")
    t = lax.axis_index("tile")
    even = lax.rem(t, 2) == 0
    at_even = pl.multiple_of(jnp.where(even, PATCH - RIM, 0), RIM)
    at_odd = pl.multiple_of(jnp.where(even, 0, PATCH - RIM), RIM)
    no_odd = jnp.logical_or(t == 0, t == tile_count - 1)
    keep = jnp.where(no_odd, 0.0, 1.0).astype(bf16)
    centers = [eq.at[0], eq.at[1], mine.at[0], mine.at[1], sib.at[0], sib.at[1]]
    slots = [0, 1, q + 2, (q ^ 2) + 2, (q ^ 1) + 2, (q ^ 3) + 2]
    for i, center in enumerate(centers):
        x_ref[i, RIM : RIM + HALF, :] = center[...]
        x_ref[i, pl.ds(at_even, RIM), :] = near[i]
        x_ref[i, pl.ds(at_odd, RIM), :] = far[i] * keep
        if i >= 2:
            offset = jnp.max(center[:16, MSG - HALF :].astype(f32))
            off_s[slots[i] - 2] = offset.astype(jnp.int32)

    lane = iota((HALF, LANES), 1)
    low = lane < HALF
    window_row = iota((QCOLS, MSG), 0)
    window_lane = iota((QCOLS, MSG), 1)
    in_window = jnp.logical_and(
        window_lane >= window_row * HALF, window_lane < window_row * HALF + PATCH
    )
    for i in range(6):
        slot = slots[i]
        x = x_ref[i]
        xf = x.astype(f32)
        column = jnp.sum(xf * xf, axis=0, keepdims=True)
        windows = jnp.sum(jnp.where(in_window, column, 0.0), axis=1, keepdims=True)
        energy[slot] = jnp.broadcast_to(windows, (QCOLS, LANES))
        y2 = dot(rows2[...], x)
        y = y2[:PATCH] + y2[PATCH:]
        evens, odds = [], []
        for v in range(QCOLS // 2 + 1):
            a = y[:HALF, LANES * v : LANES * (v + 1)]
            b = pltpu.roll(y[HALF:, LANES * v : LANES * (v + 1)], HALF, 1)
            g = jnp.where(low, a, b)
            evens.append(g)
            row0[16 * i + 2 * v : 16 * i + 2 * v + 1, :] = g[0:1]
            if v < QCOLS // 2:
                g = jnp.where(low, b, a)
                odds.append(g)
                row0[16 * i + 2 * v + 1 : 16 * i + 2 * v + 2, :] = pltpu.roll(g[0:1], HALF, 1)
        row0[16 * i + QCOLS + 1 : 16 * i + 16, :] = jnp.zeros((7, LANES), f32)
        gh, gl = split(jnp.concatenate(evens, axis=0))
        de = dot(jnp.concatenate([gh, gl], axis=1), fwd[0:256]) + dot(gh, fwd[256:384])
        gh, gl = split(jnp.concatenate(odds, axis=0))
        do = dot(jnp.concatenate([gh, gl], axis=1), fwd[384:640]) + dot(gh, fwd[640:768])
        for j in range(QCOLS):
            v = j // 2
            if j % 2 == 0:
                first, second = de[HALF * v : HALF * (v + 1)], do[HALF * v : HALF * (v + 1)]
            else:
                first, second = do[HALF * v : HALF * (v + 1)], de[HALF * (v + 1) : HALF * (v + 2)]
            spec[slot, j] = first + second

    edges = row0[...]
    edges = jnp.concatenate([edges, pltpu.roll(edges, HALF, 1)], axis=0)[:, :HALF]
    d0 = dot3(edges, fwd[0:HALF], fwd[256 : 256 + HALF])
    flip = (iota(d0.shape, 0) & iota(d0.shape, 1) & 1) == 1
    d0 = jnp.where(flip, -d0, d0)
    for i in range(6):
        for h in range(2):
            first = 96 * h + 16 * i
            spec0[slots[i], h] = d0[first : first + QCOLS] + d0[first + 1 : first + QCOLS + 1]
    products = []
    prior = []
    for s in range(SECTIONS):
        prev = s + 2 - off_s[s]
        prior.append(prev)
        for h in range(2):
            f, g = spec0[s + 2, h], spec0[prev, h]
            fr, fi = f[:, :PATCH], f[:, PATCH:]
            gr, gi = g[:, :PATCH], g[:, PATCH:]
            products.append(jnp.concatenate([fr * gr + fi * gi, fi * gr - fr * gi], axis=1))
    u0 = dot3(jnp.concatenate(products, axis=0), inv2[0:256, 0:PATCH], inv2[256:512, 0:PATCH])

    lane1 = iota((1, LANES), 1)
    shift_lane = jnp.where(lane1 < HALF, lane1, lane1 - PATCH).astype(f32)
    sub8 = iota((8, LANES), 0).astype(f32)
    scales = []
    for s in range(SECTIONS):
        prev = prior[s]
        scale8 = score_scale / jnp.sqrt(energy[s + 2] * energy[prev] + 1e-6)
        scales.append(scale8)
        highs, lows = [], []
        for j in range(QCOLS):
            f, g = spec[s + 2, j], spec[prev, j]
            fr, fi = f[:, :PATCH], f[:, PATCH:]
            gr, gi = g[:, :PATCH], g[:, PATCH:]
            ph, plo = split(jnp.concatenate([fr * gr + fi * gi, fi * gr - fr * gi], axis=1))
            highs.append(ph)
            lows.append(plo)
        ph, plo = jnp.concatenate(highs, axis=0), jnp.concatenate(lows, axis=0)
        u = dot(ph, inv2[0:256]) + dot(plo, inv2[0:256]) + dot(ph, inv2[256:512])
        for j in range(QCOLS):
            u_ref[s, j] = u[HALF * j : HALF * (j + 1)]
            first = 2 * QCOLS * s + j
            u_ref[s, j, 0:1, :PATCH] = u0[first : first + 1]
            u_ref[s, j, 0:1, PATCH:] = u0[first + QCOLS : first + QCOLS + 1]
        for j in range(0, QCOLS, 2):
            sides = []
            for k in (j, j + 1):
                uh, ul = split(u_ref[s, k])
                sides.append(
                    jnp.concatenate([uh[:, :PATCH], uh[:, PATCH:], ul[:, :PATCH], ul[:, PATCH:]], axis=0)
                )
            c2 = dot(back2[...], jnp.concatenate(sides, axis=1))
            both = c2[:PATCH] + c2[PATCH:]
            for k in (j, j + 1):
                c = both[:, PATCH * (k - j) : PATCH * (k - j + 1)]
                top = jnp.max(jnp.max(c, axis=0, keepdims=True), axis=1, keepdims=True)
                rate = scale8[k : k + 1, :]
                w = jnp.exp((c - top) * rate)
                total = w[0:8]
                moment = jnp.zeros((8, LANES), f32)
                for a in range(1, PATCH // 8):
                    block = w[8 * a : 8 * a + 8]
                    total = total + block
                    moment = moment + block * float(8 * a if 8 * a < HALF else 8 * a - PATCH)
                moment = moment + total * sub8
                total = jnp.sum(total, axis=0, keepdims=True)
                part[k, s : s + 1, :] = jnp.sum(moment, axis=0, keepdims=True)
                part[k, 4 + s : 5 + s, :] = total * shift_lane
                part[k, 8 + s : 9 + s, :] = total
                peak[k, s : s + 1, :] = jnp.broadcast_to(top, (1, LANES))

    lane16 = iota((FEATS, LANES), 1)
    lane4 = iota((SECTIONS, LANES), 1)
    lane8 = iota((QCOLS, LANES), 1)
    first_lane = q * QCOLS
    sums = jnp.zeros((FEATS, LANES), f32)
    tops = jnp.zeros((SECTIONS, LANES), f32)
    for j in range(QCOLS):
        part[j, 12:16, :] = jnp.zeros((4, LANES), f32)
        sums = sums + jnp.where(
            lane16 == first_lane + j, jnp.sum(part[j], axis=1, keepdims=True), 0.0
        )
        tops = tops + jnp.where(lane4 == first_lane + j, peak[j], 0.0)
    pick = lane8 == first_lane + iota((QCOLS, LANES), 0)
    rates = jnp.concatenate(
        [jnp.sum(jnp.where(pick, scale8, 0.0), axis=0, keepdims=True) for scale8 in scales], axis=0
    )
    mine = jnp.logical_and(lane4 >= first_lane, lane4 < first_lane + QCOLS)
    total = jnp.where(mine, sums[8:12], 1.0)
    out[0:4, :] = sums[0:4] / total
    out[4:8, :] = sums[4:8] / total
    out[8:12, :] = jnp.where(mine, (tops * rates + jnp.log(total)) / score_scale, 0.0)
    row4 = iota((SECTIONS, LANES), 0)
    flags = jnp.concatenate(
        [valid[0].astype(f32), jnp.broadcast_to(off[...], (1, COLS)), jnp.zeros((1, HALF), f32)],
        axis=1,
    )
    out[12:16, :] = jnp.where(row4 == q, flags, 0.0)


def relax_kernel(tile_count, mine, sib, flows_out, conf_out, pos_out):
    q = lax.axis_index("sec")
    t = lax.axis_index("tile")
    even = lax.rem(t, 2) == 0
    step = jnp.where(even, 1, -1)
    inside = lambda row: jnp.logical_and(row >= 0, row < tile_count)
    bundle = jnp.where(lax.rem(q, 2) == 1, mine[...], sib[...])
    own, near, far, beyond, third = [bundle[i] for i in range(5)]
    rows = [beyond, far, own, near, third]
    shape = (2 * SECTIONS, LANES)
    lane = iota(shape, 1)
    row = iota(shape, 0)
    sec = lax.rem(row, SECTIONS)
    live = lane < COLS
    offsets = jnp.max(
        jnp.where(iota((SECTIONS, LANES), 1) >= COLS, own[12:16], 0.0), axis=1, keepdims=True
    )
    offsets = jnp.broadcast_to(jnp.concatenate([offsets, offsets], axis=0), shape)
    one = offsets < 1.5
    flows, stiff, present = [], [], []
    for i, cells in enumerate(rows):
        ok = jnp.logical_and(live, inside(t + step * (i - 2)))
        present.append(ok)
        flows.append(jnp.where(ok, cells[0:8], 0.0))
        stiffness = cells[8:12] * cells[12:16]
        stiff.append(jnp.where(ok, jnp.concatenate([stiffness, stiffness], axis=0), 0.0))

    def back(x, n):
        return jnp.where(sec >= n, pltpu.roll(x, n, 0), 0.0)

    def ahead(x, n):
        return jnp.where(sec < SECTIONS - n, pltpu.roll(x, 2 * SECTIONS - n, 0), 0.0)

    zero = jnp.zeros(shape, f32)
    positions = [zero] * 5
    for iteration in range(STEPS):
        new = list(positions)
        for i in range(iteration, 5 - iteration):
            p = positions[i]
            if iteration == 0:
                tension = stiff[i] * flows[i]
                bending = zero
            else:
                pulled = jnp.where(one, back(p, 1), back(p, 2))
                tension = stiff[i] * (p - pulled + flows[i])
                bending = (
                    4.0 * p
                    - positions[i - 1]
                    - positions[i + 1]
                    - pltpu.roll(p, 1, 1)
                    - pltpu.roll(p, LANES - 1, 1)
                )
            returned = ahead(jnp.where(one, tension, 0.0), 1) + ahead(jnp.where(one, 0.0, tension), 2)
            gradient = tension - returned + plane_weight * bending
            new[i] = jnp.where(present[i], p - spring_rate * gradient, 0.0)
        positions = new
    for c in range(2):
        chosen = row == q + SECTIONS * c
        flows_out[0, c] = jnp.sum(jnp.where(chosen, flows[2], 0.0), axis=0, keepdims=True)[:, :COLS]
        pos_out[0, c] = jnp.sum(jnp.where(chosen, positions[2], 0.0), axis=0, keepdims=True)[:, :COLS]
    chosen = iota((SECTIONS, LANES), 0) == q
    conf_out[0] = jnp.sum(jnp.where(chosen, own[8:12], 0.0), axis=0, keepdims=True)[:, :COLS]


def xor_route(count, d):
    return [(i, i ^ d) for i in range(count)]


def joint_route(tile_count, odd):
    route = []
    for s in range(SECTIONS):
        for t in range(tile_count):
            to = t ^ 1 if not odd else t + (1 if t % 2 else -1)
            pair = (s, to) if 0 <= to < tile_count else (s ^ 1, t)
            route.append((s * tile_count + t, pair[0] * tile_count + pair[1]))
    return route


def gather_route(tile_count, kind):
    route = []
    for s in range(SECTIONS):
        for t in range(tile_count):
            pair = (s, t ^ 1)
            if s % 2 == 1 and kind == "z":
                pair = (s ^ 2, t)
            if s % 2 == 1 and kind == "odd":
                to = t + (1 if t % 2 else -1)
                pair = (s, to) if 0 <= to < tile_count else (s ^ 2, t)
            route.append((s * tile_count + t, pair[0] * tile_count + pair[1]))
    return route


def per_device(sections, earlier, offsets, patch_valid):
    tile_count = lax.axis_size("tile")
    q = lax.axis_index("sec")
    t = lax.axis_index("tile")
    even = t % 2 == 0
    swap = functools.partial(lax.ppermute, axis_name=("sec", "tile"))
    swap_even = functools.partial(swap, perm=joint_route(tile_count, False))
    swap_odd = functools.partial(swap, perm=joint_route(tile_count, True))
    right = 2 * QPIX * (SECTIONS // 2 - 1) + HALF_MSG - RIM - COLS * HALF
    offset = offsets.astype(bf16)[0]
    wide = jnp.pad(sections[0], ((0, 0), (RIM, right)))
    half_lane = lax.broadcasted_iota(jnp.int32, (HALF, HALF_MSG), 1)

    def half(h):
        cut = lax.dynamic_slice_in_dim(wide, 2 * QPIX * h, HALF_MSG, axis=1)
        return jnp.where(half_lane >= HALF_MSG - HALF, offset, cut)

    own = half(q // 2)
    across = lax.ppermute(half(1 - q // 2), "sec", xor_route(SECTIONS, 2))

    def quarter(strip, c):
        cut = lax.dynamic_slice_in_dim(strip, QPIX * c, MSG - HALF, axis=1)
        return jnp.concatenate([cut, strip[:, HALF_MSG - HALF :]], axis=1)

    def quarters(c):
        return jnp.stack([quarter(own, c), quarter(across, c)])

    core = q % 2
    mine = quarters(core)
    sib = lax.ppermute(quarters(1 - core), "sec", xor_route(SECTIONS, 1))
    eq = lax.dynamic_slice_in_dim(
        jnp.pad(earlier, ((0, 0), (0, 0), (RIM, right))), QPIX * q, MSG, axis=2
    )
    to_even = jnp.where(even, RIM, 0)
    to_odd = jnp.where(even, 0, RIM)

    def rows(start):
        return jnp.concatenate(
            [lax.dynamic_slice_in_dim(x, start, RIM, axis=1) for x in (eq, mine, sib)], axis=0
        )

    far = swap_odd(rows(to_odd))
    near = swap_even(rows(to_even))
    vmem = pl.BlockSpec(memory_space=pltpu.VMEM)
    consts = [jnp.asarray(x) for x in tables()]
    cells = pl.pallas_call(
        functools.partial(correlate_kernel, tile_count),
        out_shape=jax.ShapeDtypeStruct((FEATS, LANES), f32),
        in_specs=[vmem] * 11,
        out_specs=vmem,
        scratch_shapes=[
            pltpu.VMEM((6, PATCH, MSG), bf16),
            pltpu.VMEM((6, QCOLS, HALF, 256), f32),
            pltpu.VMEM((6, 2, QCOLS, 256), f32),
            pltpu.VMEM((96, LANES), f32),
            pltpu.VMEM((6, QCOLS, LANES), f32),
            pltpu.VMEM((SECTIONS, QCOLS, HALF, 256), f32),
            pltpu.VMEM((QCOLS, FEATS, LANES), f32),
            pltpu.VMEM((QCOLS, SECTIONS, LANES), f32),
            pltpu.SMEM((SECTIONS,), jnp.int32),
        ],
        compiler_params=pltpu.CompilerParams(vmem_limit_bytes=48 * 1024 * 1024),
        name="correlate",
    )(mine, sib, eq, near, far, patch_valid, offsets.astype(f32)[None], *consts)
    cells = cells + lax.ppermute(cells, "sec", xor_route(SECTIONS, 1))
    cells = cells + swap(cells, perm=gather_route(tile_count, "z"))
    near = swap(cells, perm=gather_route(tile_count, "even"))
    far = swap(jnp.stack([cells, near]), perm=gather_route(tile_count, "odd"))
    third = swap(far[0], perm=gather_route(tile_count, "even"))
    bundle = jnp.stack([cells, near, far[0], far[1], third])
    shared = lax.ppermute(bundle, "sec", xor_route(SECTIONS, 1))
    return pl.pallas_call(
        functools.partial(relax_kernel, tile_count),
        out_shape=(
            jax.ShapeDtypeStruct((1, 2, 1, COLS), f32),
            jax.ShapeDtypeStruct((1, 1, COLS), f32),
            jax.ShapeDtypeStruct((1, 2, 1, COLS), f32),
        ),
        in_specs=[vmem] * 2,
        out_specs=(vmem,) * 3,
        compiler_params=pltpu.CompilerParams(vmem_limit_bytes=8 * 1024 * 1024),
        name="relax",
    )(bundle, shared)


def solution(mesh):
    in_specs = (P("sec", "tile", None), P(None, "tile", None), P("sec"), P("sec", "tile", None))
    out_specs = (P("sec", None, "tile", None), P("sec", "tile", None), P("sec", None, "tile", None))
    return jax.shard_map(
        per_device, mesh=mesh, in_specs=in_specs, out_specs=out_specs, check_vma=False
    )
```

```python
import functools

import jax
import jax.numpy as jnp
import ml_dtypes
import numpy as np
from jax import lax
from jax.experimental import pallas as pl
from jax.experimental.pallas import tpu as pltpu
from jax.sharding import PartitionSpec as P

PATCH = 128
HALF = PATCH // 2
RIM = HALF // 2
STEPS = 3
SECTIONS = 4
COLS = 32
QCOLS = COLS // SECTIONS
QPIX = QCOLS * HALF
MSG = QPIX + PATCH
LANES = 128
FEATS = 16

score_scale = 800.0
spring_rate = 0.3
plane_weight = 0.5
f32 = jnp.float32
bf16 = jnp.bfloat16


def split_table(table):
    hi = table.astype(ml_dtypes.bfloat16)
    lo = (table - hi.astype(np.float64)).astype(ml_dtypes.bfloat16)
    return hi, lo


@functools.cache
def tables():
    n = np.arange(PATCH)
    angle = 2.0 * np.pi / PATCH * (np.outer(n, n) % PATCH)
    c, s = np.cos(angle), np.sin(angle)
    c[np.abs(c) < 1e-12] = 0.0
    s[np.abs(s) < 1e-12] = 0.0
    alt = (-1.0) ** n
    rows = np.concatenate([c[:HALF], alt[None], s[1:HALF]], axis=0)
    rows_hi, rows_lo = split_table(rows)
    rows2 = np.concatenate([rows_hi, rows_lo], axis=0)
    cols_cos = np.concatenate([c[:HALF], -s[:HALF]], axis=1)
    cols_sin = np.concatenate([-s[:HALF], -c[:HALF]], axis=1)
    even = np.concatenate([cols_cos, cols_sin], axis=0)
    odd = np.concatenate([cols_sin, cols_cos], axis=0) * np.concatenate([alt, alt])[None]
    even_hi, even_lo = split_table(even)
    odd_hi, odd_lo = split_table(odd)
    fwd = np.concatenate([even_hi, even_hi, even_lo, odd_hi, odd_hi, odd_lo], axis=0)
    inv = np.concatenate(
        [np.concatenate([c, s], axis=1), np.concatenate([-s, c], axis=1)], axis=0
    )
    inv2 = np.concatenate(split_table(inv), axis=0)
    back = np.concatenate([2.0 * c[:, :HALF], -2.0 * s[:, :HALF]], axis=1)
    back[:, 0] = 1.0
    back[:, HALF] = alt
    back_hi, back_lo = split_table(back / (PATCH * PATCH))
    back2 = np.concatenate(
        [np.concatenate([back_hi, back_hi], axis=1), np.concatenate([back_lo, back_lo], axis=1)],
        axis=0,
    )
    return (
        rows2,
        fwd,
        inv2,
        back2,
    )


def dot(a, b):
    return jnp.dot(a, b, preferred_element_type=f32)


def split(x):
    hi = x.astype(bf16)
    return hi, (x - hi.astype(f32)).astype(bf16)


def dot3(x, hi, lo):
    xh, xl = split(x)
    return dot(xh, hi) + dot(xl, hi) + dot(xh, lo)


def iota(shape, dim):
    return lax.broadcasted_iota(jnp.int32, shape, dim)


def prepare_kernel(strip, off, keep, send, wide):
    q = lax.axis_index("sec")
    h, c = lax.div(q, 2), lax.rem(q, 2)
    blank = jnp.zeros((HALF, LANES), bf16)
    wide[:, :LANES] = blank
    wide[:, LANES : LANES + COLS * HALF] = strip[0]
    wide[:, LANES + COLS * HALF :] = blank
    offset = off[0].astype(f32)
    marked = iota((HALF, MSG), 1) >= MSG - HALF
    for out, core in ((keep, c), (send, 1 - c)):
        for i, side in enumerate((h, 1 - h)):
            start = pl.multiple_of(QPIX * (2 * side + core), LANES)
            cut = wide[:, pl.ds(start, MSG + LANES)].astype(f32)
            cut = pltpu.roll(cut, MSG + RIM, 1)[:, :MSG]
            out[i] = jnp.where(marked, offset, cut).astype(bf16)


def place(x_ref, i, center, near, far, tile_count):
    t = lax.axis_index("tile")
    even = lax.rem(t, 2) == 0
    at_even = pl.multiple_of(jnp.where(even, PATCH - RIM, 0), RIM)
    at_odd = pl.multiple_of(jnp.where(even, 0, PATCH - RIM), RIM)
    no_odd = jnp.logical_or(t == 0, t == tile_count - 1)
    keep = jnp.where(no_odd, 0.0, 1.0).astype(bf16)
    x_ref[i, RIM : RIM + HALF, :] = center
    x_ref[i, pl.ds(at_even, RIM), :] = near
    x_ref[i, pl.ds(at_odd, RIM), :] = far * keep


def transform(x_ref, row0, count, rows2, fwd, spec_at, edge_at, energy_at):
    lane = iota((HALF, LANES), 1)
    low = lane < HALF
    window_row = iota((QCOLS, MSG), 0)
    window_lane = iota((QCOLS, MSG), 1)
    in_window = jnp.logical_and(
        window_lane >= window_row * HALF, window_lane < window_row * HALF + PATCH
    )
    for i in range(count):
        x = x_ref[i]
        xf = x.astype(f32)
        column = jnp.sum(xf * xf, axis=0, keepdims=True)
        windows = jnp.sum(jnp.where(in_window, column, 0.0), axis=1, keepdims=True)
        energy_at(i)[...] = jnp.broadcast_to(windows, (QCOLS, LANES))
        y2 = dot(rows2[...], x)
        y = y2[:PATCH] + y2[PATCH:]
        evens, odds = [], []
        for v in range(QCOLS // 2 + 1):
            a = y[:HALF, LANES * v : LANES * (v + 1)]
            b = pltpu.roll(y[HALF:, LANES * v : LANES * (v + 1)], HALF, 1)
            g = jnp.where(low, a, b)
            evens.append(g)
            row0[16 * i + 2 * v : 16 * i + 2 * v + 1, :] = g[0:1]
            if v < QCOLS // 2:
                g = jnp.where(low, b, a)
                odds.append(g)
                row0[16 * i + 2 * v + 1 : 16 * i + 2 * v + 2, :] = pltpu.roll(g[0:1], HALF, 1)
        row0[16 * i + QCOLS + 1 : 16 * i + 16, :] = jnp.zeros((7, LANES), f32)
        gh, gl = split(jnp.concatenate(evens, axis=0))
        de = dot(jnp.concatenate([gh, gl], axis=1), fwd[0:256]) + dot(gh, fwd[256:384])
        gh, gl = split(jnp.concatenate(odds, axis=0))
        do = dot(jnp.concatenate([gh, gl], axis=1), fwd[384:640]) + dot(gh, fwd[640:768])
        for j in range(QCOLS):
            v = j // 2
            if j % 2 == 0:
                first, second = de[HALF * v : HALF * (v + 1)], do[HALF * v : HALF * (v + 1)]
            else:
                first, second = do[HALF * v : HALF * (v + 1)], de[HALF * (v + 1) : HALF * (v + 2)]
            spec_at(i)[j] = first + second
    edges = row0[...]
    edges = jnp.concatenate([edges, pltpu.roll(edges, HALF, 1)], axis=0)[:, :HALF]
    d0 = dot3(edges, fwd[0:HALF], fwd[256 : 256 + HALF])
    flip = (iota(d0.shape, 0) & iota(d0.shape, 1) & 1) == 1
    d0 = jnp.where(flip, -d0, d0)
    for i in range(count):
        for h in range(2):
            first = 16 * count * h + 16 * i
            edge_at(i)[h] = d0[first : first + QCOLS] + d0[first + 1 : first + QCOLS + 1]


def early_kernel(
    tile_count, eq, keep, sib, near, far, rows2, fwd, spec, edge, energy, x_ref, row0
):
    centers = [eq[0], eq[1], keep[0], sib[0]]
    for i, center in enumerate(centers):
        place(x_ref, i, center, near[i], far[i], tile_count)
    transform(
        x_ref, row0, 4, rows2, fwd,
        lambda i: spec.at[i], lambda i: edge.at[i], lambda i: energy.at[i],
    )


def correlate_kernel(
    tile_count,
    spec_in, edge_in, energy_in, keep, sib, across, near, far, valid, off,
    rows2, fwd, inv2, back2,
    out,
    x_ref, spec, spec0, row0, energy, u_ref, part, peak, off_s, sems,
):
    q = lax.axis_index("sec")
    slots = [0, 1, q + 2, (q ^ 1) + 2, (q ^ 2) + 2, (q ^ 3) + 2]
    copies = [
        pltpu.make_async_copy(spec_in.at[i], spec.at[slots[i]], sems.at[i]) for i in range(4)
    ]
    for copy in copies:
        copy.start()
    for i in range(4):
        spec0[slots[i]] = edge_in[i]
        energy[slots[i]] = energy_in[i]
    for i, center in enumerate((keep.at[0], sib.at[0], across.at[0], across.at[1])):
        offset = jnp.max(center[:16, MSG - HALF :].astype(f32))
        off_s[slots[2 + i] - 2] = offset.astype(jnp.int32)
    for i in range(2):
        place(x_ref, i, across[i], near[i], far[i], tile_count)
    transform(
        x_ref, row0, 2, rows2, fwd,
        lambda i: spec.at[slots[4 + i]],
        lambda i: spec0.at[slots[4 + i]],
        lambda i: energy.at[slots[4 + i]],
    )

    products = []
    prior = []
    for s in range(SECTIONS):
        prev = s + 2 - off_s[s]
        prior.append(prev)
        for h in range(2):
            f, g = spec0[s + 2, h], spec0[prev, h]
            fr, fi = f[:, :PATCH], f[:, PATCH:]
            gr, gi = g[:, :PATCH], g[:, PATCH:]
            products.append(jnp.concatenate([fr * gr + fi * gi, fi * gr - fr * gi], axis=1))
    u0 = dot3(jnp.concatenate(products, axis=0), inv2[0:256, 0:PATCH], inv2[256:512, 0:PATCH])
    for copy in copies:
        copy.wait()

    lane1 = iota((1, LANES), 1)
    shift_lane = jnp.where(lane1 < HALF, lane1, lane1 - PATCH).astype(f32)
    sub8 = iota((8, LANES), 0).astype(f32)
    scales = []
    for s in range(SECTIONS):
        prev = prior[s]
        scale8 = score_scale / jnp.sqrt(energy[s + 2] * energy[prev] + 1e-6)
        scales.append(scale8)
        first = 2 * QCOLS * s
        edge_rows = jnp.concatenate(
            [u0[first : first + QCOLS], u0[first + QCOLS : first + 2 * QCOLS]], axis=1
        )
        highs, lows = [], []
        for j in range(QCOLS):
            f, g = spec[s + 2, j], spec[prev, j]
            fr, fi = f[:, :PATCH], f[:, PATCH:]
            gr, gi = g[:, :PATCH], g[:, PATCH:]
            ph, plo = split(jnp.concatenate([fr * gr + fi * gi, fi * gr - fr * gi], axis=1))
            highs.append(ph)
            lows.append(plo)
        ph, plo = jnp.concatenate(highs, axis=0), jnp.concatenate(lows, axis=0)
        u = dot(ph, inv2[0:256]) + dot(plo, inv2[0:256]) + dot(ph, inv2[256:512])
        for j in range(QCOLS):
            u_ref[s, j] = u[HALF * j : HALF * (j + 1)]
            u_ref[s, j, 0:1, :] = edge_rows[j : j + 1]
        for j in range(0, QCOLS, 2):
            sides = []
            for k in (j, j + 1):
                uh, ul = split(u_ref[s, k])
                sides.append(
                    jnp.concatenate([uh[:, :PATCH], uh[:, PATCH:], ul[:, :PATCH], ul[:, PATCH:]], axis=0)
                )
            c2 = dot(back2[...], jnp.concatenate(sides, axis=1))
            both = c2[:PATCH] + c2[PATCH:]
            for k in (j, j + 1):
                c = both[:, PATCH * (k - j) : PATCH * (k - j + 1)]
                top = jnp.max(jnp.max(c, axis=0, keepdims=True), axis=1, keepdims=True)
                rate = scale8[k : k + 1, :]
                w = jnp.exp((c - top) * rate)
                total = w[0:8]
                moment = jnp.zeros((8, LANES), f32)
                for a in range(1, PATCH // 8):
                    block = w[8 * a : 8 * a + 8]
                    total = total + block
                    moment = moment + block * float(8 * a if 8 * a < HALF else 8 * a - PATCH)
                moment = moment + total * sub8
                total = jnp.sum(total, axis=0, keepdims=True)
                part[k, s : s + 1, :] = jnp.sum(moment, axis=0, keepdims=True)
                part[k, 4 + s : 5 + s, :] = total * shift_lane
                part[k, 8 + s : 9 + s, :] = total
                peak[k, s : s + 1, :] = jnp.broadcast_to(top, (1, LANES))

    lane16 = iota((FEATS, LANES), 1)
    lane4 = iota((SECTIONS, LANES), 1)
    lane8 = iota((QCOLS, LANES), 1)
    first_lane = q * QCOLS
    sums = jnp.zeros((FEATS, LANES), f32)
    tops = jnp.zeros((SECTIONS, LANES), f32)
    for j in range(QCOLS):
        part[j, 12:16, :] = jnp.zeros((4, LANES), f32)
        sums = sums + jnp.where(
            lane16 == first_lane + j, jnp.sum(part[j], axis=1, keepdims=True), 0.0
        )
        tops = tops + jnp.where(lane4 == first_lane + j, peak[j], 0.0)
    pick = lane8 == first_lane + iota((QCOLS, LANES), 0)
    rates = jnp.concatenate(
        [jnp.sum(jnp.where(pick, scale8, 0.0), axis=0, keepdims=True) for scale8 in scales], axis=0
    )
    mine = jnp.logical_and(lane4 >= first_lane, lane4 < first_lane + QCOLS)
    total = jnp.where(mine, sums[8:12], 1.0)
    out[0:4, :] = sums[0:4] / total
    out[4:8, :] = sums[4:8] / total
    out[8:12, :] = jnp.where(mine, (tops * rates + jnp.log(total)) / score_scale, 0.0)
    row4 = iota((SECTIONS, LANES), 0)
    flags = jnp.concatenate(
        [valid[0].astype(f32), jnp.broadcast_to(off[...], (1, COLS)), jnp.zeros((1, HALF), f32)],
        axis=1,
    )
    out[12:16, :] = jnp.where(row4 == q, flags, 0.0)


def relax_kernel(tile_count, mine, sib, flows_out, conf_out, pos_out):
    q = lax.axis_index("sec")
    t = lax.axis_index("tile")
    even = lax.rem(t, 2) == 0
    step = jnp.where(even, 1, -1)
    inside = lambda row: jnp.logical_and(row >= 0, row < tile_count)
    bundle = jnp.where(lax.rem(q, 2) == 1, mine[...], sib[...])
    own, near, far, beyond, third = [bundle[i] for i in range(5)]
    rows = [beyond, far, own, near, third]
    shape = (2 * SECTIONS, LANES)
    lane = iota(shape, 1)
    row = iota(shape, 0)
    sec = lax.rem(row, SECTIONS)
    live = lane < COLS
    offsets = jnp.max(
        jnp.where(iota((SECTIONS, LANES), 1) >= COLS, own[12:16], 0.0), axis=1, keepdims=True
    )
    offsets = jnp.broadcast_to(jnp.concatenate([offsets, offsets], axis=0), shape)
    one = offsets < 1.5
    flows, stiff, present = [], [], []
    for i, cells in enumerate(rows):
        ok = jnp.logical_and(live, inside(t + step * (i - 2)))
        present.append(ok)
        flows.append(jnp.where(ok, cells[0:8], 0.0))
        stiffness = cells[8:12] * cells[12:16]
        stiff.append(jnp.where(ok, jnp.concatenate([stiffness, stiffness], axis=0), 0.0))

    def back(x, n):
        return jnp.where(sec >= n, pltpu.roll(x, n, 0), 0.0)

    def ahead(x, n):
        return jnp.where(sec < SECTIONS - n, pltpu.roll(x, 2 * SECTIONS - n, 0), 0.0)

    zero = jnp.zeros(shape, f32)
    positions = [zero] * 5
    for iteration in range(STEPS):
        new = list(positions)
        for i in range(iteration, 5 - iteration):
            p = positions[i]
            if iteration == 0:
                tension = stiff[i] * flows[i]
                bending = zero
            else:
                pulled = jnp.where(one, back(p, 1), back(p, 2))
                tension = stiff[i] * (p - pulled + flows[i])
                bending = (
                    4.0 * p
                    - positions[i - 1]
                    - positions[i + 1]
                    - pltpu.roll(p, 1, 1)
                    - pltpu.roll(p, LANES - 1, 1)
                )
            returned = ahead(jnp.where(one, tension, 0.0), 1) + ahead(jnp.where(one, 0.0, tension), 2)
            gradient = tension - returned + plane_weight * bending
            new[i] = jnp.where(present[i], p - spring_rate * gradient, 0.0)
        positions = new
    for c in range(2):
        chosen = row == q + SECTIONS * c
        flows_out[0, c] = jnp.sum(jnp.where(chosen, flows[2], 0.0), axis=0, keepdims=True)[:, :COLS]
        pos_out[0, c] = jnp.sum(jnp.where(chosen, positions[2], 0.0), axis=0, keepdims=True)[:, :COLS]
    chosen = iota((SECTIONS, LANES), 0) == q
    conf_out[0] = jnp.sum(jnp.where(chosen, own[8:12], 0.0), axis=0, keepdims=True)[:, :COLS]


def xor_route(count, d):
    return [(i, i ^ d) for i in range(count)]


def joint_route(tile_count, odd):
    route = []
    for s in range(SECTIONS):
        for t in range(tile_count):
            to = t ^ 1 if not odd else t + (1 if t % 2 else -1)
            pair = (s, to) if 0 <= to < tile_count else (s ^ 1, t)
            route.append((s * tile_count + t, pair[0] * tile_count + pair[1]))
    return route


def gather_route(tile_count, kind):
    route = []
    for s in range(SECTIONS):
        for t in range(tile_count):
            pair = (s, t ^ 1)
            if s % 2 == 1 and kind == "z":
                pair = (s ^ 2, t)
            if s % 2 == 1 and kind == "odd":
                to = t + (1 if t % 2 else -1)
                pair = (s, to) if 0 <= to < tile_count else (s ^ 2, t)
            route.append((s * tile_count + t, pair[0] * tile_count + pair[1]))
    return route


def per_device(sections, earlier, offsets, patch_valid):
    tile_count = lax.axis_size("tile")
    q = lax.axis_index("sec")
    t = lax.axis_index("tile")
    even = t % 2 == 0
    swap = functools.partial(lax.ppermute, axis_name=("sec", "tile"))
    swap_even = functools.partial(swap, perm=joint_route(tile_count, False))
    swap_odd = functools.partial(swap, perm=joint_route(tile_count, True))
    vmem = pl.BlockSpec(memory_space=pltpu.VMEM)
    smem = pl.BlockSpec(memory_space=pltpu.SMEM)
    quarters = jax.ShapeDtypeStruct((2, HALF, MSG), bf16)
    keep, send = pl.pallas_call(
        prepare_kernel,
        out_shape=(quarters, quarters),
        in_specs=[vmem, smem],
        out_specs=(vmem, vmem),
        scratch_shapes=[pltpu.VMEM((HALF, 2 * LANES + COLS * HALF), bf16)],
        compiler_params=pltpu.CompilerParams(vmem_limit_bytes=8 * 1024 * 1024),
        name="prepare",
    )(sections, offsets)
    sib = lax.ppermute(send, "sec", xor_route(SECTIONS, 1))
    across = lax.ppermute(jnp.stack([keep[1], sib[1]]), "sec", xor_route(SECTIONS, 2))
    right = QPIX * (SECTIONS - 1) + MSG - RIM - COLS * HALF
    eq = lax.dynamic_slice_in_dim(
        jnp.pad(earlier, ((0, 0), (0, 0), (RIM, right))), QPIX * q, MSG, axis=2
    )
    to_even = jnp.where(even, RIM, 0)
    to_odd = jnp.where(even, 0, RIM)

    def rows(images, start):
        return jnp.concatenate(
            [lax.dynamic_slice_in_dim(x, start, RIM, axis=1) for x in images], axis=0
        )

    local = (eq, keep[:1], sib[:1])
    far_local = swap_odd(rows(local, to_odd))
    near_local = swap_even(rows(local, to_even))
    far_across = swap_odd(rows((across,), to_odd))
    near_across = swap_even(rows((across,), to_even))
    rows2, fwd, inv2, back2 = [jnp.asarray(x) for x in tables()]
    spec, edge, energy = pl.pallas_call(
        functools.partial(early_kernel, tile_count),
        out_shape=(
            jax.ShapeDtypeStruct((4, QCOLS, HALF, 256), f32),
            jax.ShapeDtypeStruct((4, 2, QCOLS, 256), f32),
            jax.ShapeDtypeStruct((4, QCOLS, LANES), f32),
        ),
        in_specs=[vmem] * 7,
        out_specs=(vmem,) * 3,
        scratch_shapes=[pltpu.VMEM((4, PATCH, MSG), bf16), pltpu.VMEM((64, LANES), f32)],
        compiler_params=pltpu.CompilerParams(vmem_limit_bytes=24 * 1024 * 1024),
        name="early",
    )(eq, keep, sib, near_local, far_local, rows2, fwd)
    cells = pl.pallas_call(
        functools.partial(correlate_kernel, tile_count),
        out_shape=jax.ShapeDtypeStruct((FEATS, LANES), f32),
        in_specs=[pl.BlockSpec(memory_space=pl.ANY)] + [vmem] * 13,
        out_specs=vmem,
        scratch_shapes=[
            pltpu.VMEM((2, PATCH, MSG), bf16),
            pltpu.VMEM((6, QCOLS, HALF, 256), f32),
            pltpu.VMEM((6, 2, QCOLS, 256), f32),
            pltpu.VMEM((32, LANES), f32),
            pltpu.VMEM((6, QCOLS, LANES), f32),
            pltpu.VMEM((SECTIONS, QCOLS, HALF, 256), f32),
            pltpu.VMEM((QCOLS, FEATS, LANES), f32),
            pltpu.VMEM((QCOLS, SECTIONS, LANES), f32),
            pltpu.SMEM((SECTIONS,), jnp.int32),
            pltpu.SemaphoreType.DMA((4,)),
        ],
        compiler_params=pltpu.CompilerParams(vmem_limit_bytes=32 * 1024 * 1024),
        name="correlate",
    )(
        spec, edge, energy, keep, sib, across, near_across, far_across,
        patch_valid, offsets.astype(f32)[None], rows2, fwd, inv2, back2,
    )
    cells = cells + lax.ppermute(cells, "sec", xor_route(SECTIONS, 1))
    cells = cells + swap(cells, perm=gather_route(tile_count, "z"))
    near = swap(cells, perm=gather_route(tile_count, "even"))
    far = swap(jnp.stack([cells, near]), perm=gather_route(tile_count, "odd"))
    third = swap(far[0], perm=gather_route(tile_count, "even"))
    bundle = jnp.stack([cells, near, far[0], far[1], third])
    shared = lax.ppermute(bundle, "sec", xor_route(SECTIONS, 1))
    return pl.pallas_call(
        functools.partial(relax_kernel, tile_count),
        out_shape=(
            jax.ShapeDtypeStruct((1, 2, 1, COLS), f32),
            jax.ShapeDtypeStruct((1, 1, COLS), f32),
            jax.ShapeDtypeStruct((1, 2, 1, COLS), f32),
        ),
        in_specs=[vmem] * 2,
        out_specs=(vmem,) * 3,
        compiler_params=pltpu.CompilerParams(vmem_limit_bytes=8 * 1024 * 1024),
        name="relax",
    )(bundle, shared)


def solution(mesh):
    in_specs = (P("sec", "tile", None), P(None, "tile", None), P("sec"), P("sec", "tile", None))
    out_specs = (P("sec", None, "tile", None), P("sec", "tile", None), P("sec", None, "tile", None))
    return jax.shard_map(
        per_device, mesh=mesh, in_specs=in_specs, out_specs=out_specs, check_vma=False
    )
```

```python
import functools
import math

import jax
import jax.numpy as jnp
import ml_dtypes
import numpy as np
from jax import lax
from jax.experimental import pallas as pl
from jax.experimental.pallas import tpu as pltpu
from jax.sharding import PartitionSpec as P

PATCH = 128
HALF = PATCH // 2
RIM = HALF // 2
STEPS = 3
SECTIONS = 4
COLS = 32
QCOLS = COLS // SECTIONS
QPIX = QCOLS * HALF
MSG = QPIX + PATCH
LANES = 128
FEATS = 16

score_scale = 800.0
spring_rate = 0.3
plane_weight = 0.5
f32 = jnp.float32
bf16 = jnp.bfloat16


def split_table(table):
    hi = table.astype(ml_dtypes.bfloat16)
    lo = (table - hi.astype(np.float64)).astype(ml_dtypes.bfloat16)
    return hi, lo


@functools.cache
def tables():
    n = np.arange(PATCH)
    angle = 2.0 * np.pi / PATCH * (np.outer(n, n) % PATCH)
    c, s = np.cos(angle), np.sin(angle)
    c[np.abs(c) < 1e-12] = 0.0
    s[np.abs(s) < 1e-12] = 0.0
    alt = (-1.0) ** n
    rows = np.concatenate([c[:HALF], alt[None], s[1:HALF]], axis=0)
    rows_hi, rows_lo = split_table(rows)
    rows2 = np.concatenate([rows_hi, rows_lo], axis=1)
    cols_cos = np.concatenate([c[:HALF], -s[:HALF]], axis=1)
    cols_sin = np.concatenate([-s[:HALF], -c[:HALF]], axis=1)
    even = np.concatenate([cols_cos, cols_sin], axis=0)
    odd = np.concatenate([cols_sin, cols_cos], axis=0) * np.concatenate([alt, alt])[None]
    even_hi, even_lo = split_table(even)
    odd_hi, odd_lo = split_table(odd)
    fwd = np.concatenate([even_hi, even_hi, even_lo, odd_hi, odd_hi, odd_lo], axis=0)
    inv = np.concatenate(
        [np.concatenate([c, s], axis=1), np.concatenate([-s, c], axis=1)], axis=0
    )
    inv_hi, inv_lo = split_table(inv)
    inv3 = np.concatenate([inv_hi, inv_hi, inv_lo], axis=0)
    back = np.concatenate([2.0 * c[:, :HALF], -2.0 * s[:, :HALF]], axis=1)
    back[:, 0] = 1.0
    back[:, HALF] = alt
    back_hi, back_lo = split_table(back / (PATCH * PATCH))
    back3 = np.concatenate([back_hi, back_hi, back_lo], axis=1)
    return (
        rows2,
        fwd,
        inv3,
        back3,
    )


def dot(a, b):
    return jnp.dot(a, b, preferred_element_type=f32)


def split(x):
    hi = x.astype(bf16)
    return hi, (x - hi.astype(f32)).astype(bf16)


def dot3(x, hi, lo):
    xh, xl = split(x)
    return dot(xh, hi) + dot(xl, hi) + dot(xh, lo)


def iota(shape, dim):
    return lax.broadcasted_iota(jnp.int32, shape, dim)


def prepare_kernel(strip, off, keep, send, wide):
    q = lax.axis_index("sec")
    h, c = lax.div(q, 2), lax.rem(q, 2)
    blank = jnp.zeros((HALF, LANES), bf16)
    wide[:, :LANES] = blank
    wide[:, LANES : LANES + COLS * HALF] = strip[0]
    wide[:, LANES + COLS * HALF :] = blank
    offset = jnp.broadcast_to(off[...].astype(f32), (HALF, MSG))
    marked = iota((HALF, MSG), 1) >= MSG - HALF
    for out, core in ((send, 1 - c), (keep, c)):
        for i, side in enumerate((h, 1 - h)):
            start = pl.multiple_of(QPIX * (2 * side + core), LANES)
            cut = wide[:, pl.ds(start, MSG + LANES)].astype(f32)
            cut = pltpu.roll(cut, MSG + RIM, 1)[:, :MSG]
            out[i] = jnp.where(marked, offset, cut).astype(bf16)


def place(x_ref, i, center, near, far, tile_count):
    t = lax.axis_index("tile")
    even = lax.rem(t, 2) == 0
    at_even = pl.multiple_of(jnp.where(even, PATCH - RIM, 0), RIM)
    at_odd = pl.multiple_of(jnp.where(even, 0, PATCH - RIM), RIM)
    no_odd = jnp.logical_or(t == 0, t == tile_count - 1)
    keep = jnp.where(no_odd, 0.0, 1.0).astype(bf16)
    x_ref[i, RIM : RIM + HALF, :] = center
    x_ref[i, pl.ds(at_even, RIM), :] = near
    x_ref[i, pl.ds(at_odd, RIM), :] = far * keep


def transform(x_ref, row0, count, rows2, fwd, spec_at, edge_at, energy_at):
    lane = iota((HALF, LANES), 1)
    low = lane < HALF
    window_row = iota((QCOLS, MSG), 0)
    window_lane = iota((QCOLS, MSG), 1)
    in_window = jnp.logical_and(
        window_lane >= window_row * HALF, window_lane < window_row * HALF + PATCH
    )
    for i in range(count):
        x = x_ref[i]
        xf = x.astype(f32)
        column = jnp.sum(xf * xf, axis=0, keepdims=True)
        windows = jnp.sum(jnp.where(in_window, column, 0.0), axis=1, keepdims=True)
        energy_at(i)[...] = jnp.broadcast_to(windows, (QCOLS, LANES))
        y = dot(rows2[...], jnp.concatenate([x, x], axis=0))
        evens, odds = [], []
        for v in range(QCOLS // 2 + 1):
            a = y[:HALF, LANES * v : LANES * (v + 1)]
            b = pltpu.roll(y[HALF:, LANES * v : LANES * (v + 1)], HALF, 1)
            g = jnp.where(low, a, b)
            evens.append(g)
            row0[16 * i + 2 * v : 16 * i + 2 * v + 1, :] = g[0:1]
            if v < QCOLS // 2:
                g = jnp.where(low, b, a)
                odds.append(g)
                row0[16 * i + 2 * v + 1 : 16 * i + 2 * v + 2, :] = pltpu.roll(g[0:1], HALF, 1)
        row0[16 * i + QCOLS + 1 : 16 * i + 16, :] = jnp.zeros((7, LANES), f32)
        gh, gl = split(jnp.concatenate(evens, axis=0))
        de = dot(jnp.concatenate([gh, gl, gh], axis=1), fwd[0:384])
        gh, gl = split(jnp.concatenate(odds, axis=0))
        do = dot(jnp.concatenate([gh, gl, gh], axis=1), fwd[384:768])
        for j in range(QCOLS):
            v = j // 2
            if j % 2 == 0:
                first, second = de[HALF * v : HALF * (v + 1)], do[HALF * v : HALF * (v + 1)]
            else:
                first, second = do[HALF * v : HALF * (v + 1)], de[HALF * (v + 1) : HALF * (v + 2)]
            spec_at(i)[j] = first + second
    edges = row0[...]
    edges = jnp.concatenate([edges, pltpu.roll(edges, HALF, 1)], axis=0)[:, :HALF]
    d0 = dot3(edges, fwd[0:HALF], fwd[256 : 256 + HALF])
    flip = (iota(d0.shape, 0) & iota(d0.shape, 1) & 1) == 1
    d0 = jnp.where(flip, -d0, d0)
    for i in range(count):
        for h in range(2):
            first = 16 * count * h + 16 * i
            edge_at(i)[h] = d0[first : first + QCOLS] + d0[first + 1 : first + QCOLS + 1]


def early_kernel(
    tile_count, eq, keep, sib, near, far, rows2, fwd, spec, edge, energy, x_ref, row0
):
    centers = [eq[0], eq[1], keep[0], sib[0]]
    for i, center in enumerate(centers):
        place(x_ref, i, center, near[i], far[i], tile_count)
    transform(
        x_ref, row0, 4, rows2, fwd,
        lambda i: spec.at[i], lambda i: edge.at[i], lambda i: energy.at[i],
    )


def correlate_kernel(
    tile_count,
    spec_in, edge_in, energy_in, keep, sib, across, far, near, valid,
    rows2, fwd, inv3, back3,
    out,
    x_ref, spec, spec0, row0, energy, u_ref, c_ref, part, peak, off_s, sems,
):
    q = lax.axis_index("sec")
    slots = [0, 1, q + 2, (q ^ 1) + 2, (q ^ 2) + 2, (q ^ 3) + 2]
    copies = [
        pltpu.make_async_copy(spec_in.at[i], spec.at[slots[i]], sems.at[i]) for i in range(4)
    ]
    for copy in copies:
        copy.start()
    for i in range(4):
        spec0[slots[i]] = edge_in[i]
        energy[slots[i]] = energy_in[i]
    for i, center in enumerate((keep.at[0], sib.at[0], across.at[0], across.at[1])):
        offset = jnp.max(center[:16, MSG - HALF :].astype(f32))
        off_s[slots[2 + i] - 2] = offset.astype(jnp.int32)
    for i in range(2):
        place(x_ref, i, across[i], near[i], far[i], tile_count)
    transform(
        x_ref, row0, 2, rows2, fwd,
        lambda i: spec.at[slots[4 + i]],
        lambda i: spec0.at[slots[4 + i]],
        lambda i: energy.at[slots[4 + i]],
    )

    products = []
    prior = []
    for s in range(SECTIONS):
        prev = s + 2 - off_s[s]
        prior.append(prev)
        for h in range(2):
            f, g = spec0[s + 2, h], spec0[prev, h]
            fr, fi = f[:, :PATCH], f[:, PATCH:]
            gr, gi = g[:, :PATCH], g[:, PATCH:]
            products.append(jnp.concatenate([fr * gr + fi * gi, fi * gr - fr * gi], axis=1))
    u0 = dot3(jnp.concatenate(products, axis=0), inv3[0:256, 0:PATCH], inv3[512:768, 0:PATCH])
    for copy in copies:
        copy.wait()

    lane1 = iota((1, LANES), 1)
    shift_lane = jnp.where(lane1 < HALF, lane1, lane1 - PATCH).astype(f32)
    sub8 = iota((8, LANES), 0).astype(f32)
    scales = []

    def inverse(s):
        prev = prior[s]
        scales.append(score_scale / jnp.sqrt(energy[s + 2] * energy[prev] + 1e-6))
        highs, lows = [], []
        for j in range(QCOLS):
            f, g = spec[s + 2, j], spec[prev, j]
            fr, fi = f[:, :PATCH], f[:, PATCH:]
            gr, gi = g[:, :PATCH], g[:, PATCH:]
            ph, plo = split(jnp.concatenate([fr * gr + fi * gi, fi * gr - fr * gi], axis=1))
            highs.append(ph)
            lows.append(plo)
        ph, plo = jnp.concatenate(highs, axis=0), jnp.concatenate(lows, axis=0)
        u = dot(jnp.concatenate([ph, plo, ph], axis=1), inv3[...])
        first = 2 * QCOLS * s
        edge_rows = jnp.concatenate(
            [u0[first : first + QCOLS], u0[first + QCOLS : first + 2 * QCOLS]], axis=1
        )
        for j in range(QCOLS):
            u_ref[s, j] = u[HALF * j : HALF * (j + 1)]
            u_ref[s, j, 0:1, :] = edge_rows[j : j + 1]

    def shifts(s):
        for j in range(0, QCOLS, 2):
            sides = []
            for k in (j, j + 1):
                uh, ul = split(u_ref[s, k])
                high = [uh[:, :PATCH], uh[:, PATCH:]]
                sides.append(
                    jnp.concatenate(high + [ul[:, :PATCH], ul[:, PATCH:]] + high, axis=0)
                )
            both = dot(back3[...], jnp.concatenate(sides, axis=1))
            for k in (j, j + 1):
                c = both[:, PATCH * (k - j) : PATCH * (k - j + 1)]
                c_ref[s % 2, k] = c
                peak[s, k : k + 1, :] = jnp.max(c, axis=0, keepdims=True)

    def soften(s):
        top8 = jnp.broadcast_to(jnp.max(peak[s], axis=1, keepdims=True), (QCOLS, LANES))
        peak[s] = top8
        rate8 = scales[s] * math.log2(math.e)
        for k in range(QCOLS):
            top = top8[k : k + 1, :]
            rate = rate8[k : k + 1, :]
            total = jnp.zeros((8, LANES), f32)
            moment = jnp.zeros((8, LANES), f32)
            for a in range(15, -1, -1):
                row = 8 * ((a + 8) % 16)
                total = total + jnp.exp2((c_ref[s % 2, k, row : row + 8, :] - top) * rate)
                if a:
                    moment = moment + total
            moment = 8.0 * moment + total * (sub8 - HALF)
            total = jnp.sum(total, axis=0, keepdims=True)
            part[k, s : s + 1, :] = jnp.sum(moment, axis=0, keepdims=True)
            part[k, 4 + s : 5 + s, :] = total * shift_lane
            part[k, 8 + s : 9 + s, :] = total

    inverse(0)
    for s in range(SECTIONS):
        if s + 1 < SECTIONS:
            inverse(s + 1)
        shifts(s)
        soften(s)

    lane16 = iota((FEATS, LANES), 1)
    lane4 = iota((SECTIONS, LANES), 1)
    lane8 = iota((QCOLS, LANES), 1)
    first_lane = q * QCOLS
    sums = jnp.zeros((FEATS, LANES), f32)
    for j in range(QCOLS):
        part[j, 12:16, :] = jnp.zeros((4, LANES), f32)
        sums = sums + jnp.where(
            lane16 == first_lane + j, jnp.sum(part[j], axis=1, keepdims=True), 0.0
        )
    pick = lane8 == first_lane + iota((QCOLS, LANES), 0)

    def gathered(rows):
        return jnp.concatenate(
            [jnp.sum(jnp.where(pick, x, 0.0), axis=0, keepdims=True) for x in rows], axis=0
        )

    rates = gathered(scales)
    tops = gathered([peak[s] for s in range(SECTIONS)])
    mine = jnp.logical_and(lane4 >= first_lane, lane4 < first_lane + QCOLS)
    total = jnp.where(mine, sums[8:12], 1.0)
    out[0:4, :] = sums[0:4] / total
    out[4:8, :] = sums[4:8] / total
    out[8:12, :] = jnp.where(mine, (tops * rates + jnp.log(total)) / score_scale, 0.0)
    row4 = iota((SECTIONS, LANES), 0)
    flags = jnp.concatenate(
        [
            valid[0].astype(f32),
            keep[0, 0:1, MSG - COLS :].astype(f32),
            jnp.zeros((1, HALF), f32),
        ],
        axis=1,
    )
    out[12:16, :] = jnp.where(row4 == q, flags, 0.0)


def relax_kernel(tile_count, mine, sib, flows_out, conf_out, pos_out):
    q = lax.axis_index("sec")
    t = lax.axis_index("tile")
    even = lax.rem(t, 2) == 0
    step = jnp.where(even, 1, -1)
    inside = lambda row: jnp.logical_and(row >= 0, row < tile_count)
    bundle = jnp.where(lax.rem(q, 2) == 1, mine[...], sib[...])
    own, near, far, beyond, third = [bundle[i] for i in range(5)]
    rows = [beyond, far, own, near, third]
    shape = (2 * SECTIONS, LANES)
    lane = iota(shape, 1)
    row = iota(shape, 0)
    sec = lax.rem(row, SECTIONS)
    live = lane < COLS
    offsets = jnp.max(
        jnp.where(iota((SECTIONS, LANES), 1) >= COLS, own[12:16], 0.0), axis=1, keepdims=True
    )
    offsets = jnp.broadcast_to(jnp.concatenate([offsets, offsets], axis=0), shape)
    one = offsets < 1.5
    flows, stiff, present = [], [], []
    for i, cells in enumerate(rows):
        ok = jnp.logical_and(live, inside(t + step * (i - 2)))
        present.append(ok)
        flows.append(jnp.where(ok, cells[0:8], 0.0))
        stiffness = cells[8:12] * cells[12:16]
        stiff.append(jnp.where(ok, jnp.concatenate([stiffness, stiffness], axis=0), 0.0))

    def back(x, n):
        return jnp.where(sec >= n, pltpu.roll(x, n, 0), 0.0)

    def ahead(x, n):
        return jnp.where(sec < SECTIONS - n, pltpu.roll(x, 2 * SECTIONS - n, 0), 0.0)

    zero = jnp.zeros(shape, f32)
    positions = [zero] * 5
    for iteration in range(STEPS):
        new = list(positions)
        for i in range(iteration, 5 - iteration):
            p = positions[i]
            if iteration == 0:
                tension = stiff[i] * flows[i]
                bending = zero
            else:
                pulled = jnp.where(one, back(p, 1), back(p, 2))
                tension = stiff[i] * (p - pulled + flows[i])
                bending = (
                    4.0 * p
                    - positions[i - 1]
                    - positions[i + 1]
                    - pltpu.roll(p, 1, 1)
                    - pltpu.roll(p, LANES - 1, 1)
                )
            returned = ahead(jnp.where(one, tension, 0.0), 1) + ahead(jnp.where(one, 0.0, tension), 2)
            gradient = tension - returned + plane_weight * bending
            new[i] = jnp.where(present[i], p - spring_rate * gradient, 0.0)
        positions = new
    for c in range(2):
        chosen = row == q + SECTIONS * c
        flows_out[0, c] = jnp.sum(jnp.where(chosen, flows[2], 0.0), axis=0, keepdims=True)[:, :COLS]
        pos_out[0, c] = jnp.sum(jnp.where(chosen, positions[2], 0.0), axis=0, keepdims=True)[:, :COLS]
    chosen = iota((SECTIONS, LANES), 0) == q
    conf_out[0] = jnp.sum(jnp.where(chosen, own[8:12], 0.0), axis=0, keepdims=True)[:, :COLS]


def xor_route(count, d):
    return [(i, i ^ d) for i in range(count)]


def joint_route(tile_count, odd):
    route = []
    for s in range(SECTIONS):
        for t in range(tile_count):
            to = t ^ 1 if not odd else t + (1 if t % 2 else -1)
            pair = (s, to) if 0 <= to < tile_count else (s ^ 1, t)
            route.append((s * tile_count + t, pair[0] * tile_count + pair[1]))
    return route


def gather_route(tile_count, kind):
    route = []
    for s in range(SECTIONS):
        for t in range(tile_count):
            pair = (s, t ^ 1)
            if s % 2 == 1 and kind == "z":
                pair = (s ^ 2, t)
            if s % 2 == 1 and kind == "odd":
                to = t + (1 if t % 2 else -1)
                pair = (s, to) if 0 <= to < tile_count else (s ^ 2, t)
            route.append((s * tile_count + t, pair[0] * tile_count + pair[1]))
    return route


def per_device(sections, earlier, offsets, patch_valid):
    tile_count = lax.axis_size("tile")
    q = lax.axis_index("sec")
    t = lax.axis_index("tile")
    even = t % 2 == 0
    swap = functools.partial(lax.ppermute, axis_name=("sec", "tile"))
    swap_even = functools.partial(swap, perm=joint_route(tile_count, False))
    swap_odd = functools.partial(swap, perm=joint_route(tile_count, True))
    vmem = pl.BlockSpec(memory_space=pltpu.VMEM)
    quarters = jax.ShapeDtypeStruct((2, HALF, MSG), bf16)
    keep, send = pl.pallas_call(
        prepare_kernel,
        out_shape=(quarters, quarters),
        in_specs=[vmem, vmem],
        out_specs=(vmem, vmem),
        scratch_shapes=[pltpu.VMEM((HALF, 2 * LANES + COLS * HALF), bf16)],
        compiler_params=pltpu.CompilerParams(vmem_limit_bytes=8 * 1024 * 1024),
        name="prepare",
    )(sections, offsets[None])
    sib = lax.ppermute(send, "sec", xor_route(SECTIONS, 1))
    across = lax.ppermute(jnp.stack([keep[1], sib[1]]), "sec", xor_route(SECTIONS, 2))
    right = QPIX * (SECTIONS - 1) + MSG - RIM - COLS * HALF
    eq = lax.dynamic_slice_in_dim(
        jnp.pad(earlier, ((0, 0), (0, 0), (RIM, right))), QPIX * q, MSG, axis=2
    )
    to_even = jnp.where(even, RIM, 0)
    to_odd = jnp.where(even, 0, RIM)

    def rows(images, start):
        return jnp.concatenate(
            [lax.dynamic_slice_in_dim(x, start, RIM, axis=1) for x in images], axis=0
        )

    local = (eq, keep[:1], sib[:1])
    far_local = swap_odd(rows(local, to_odd))
    near_local = swap_even(rows(local, to_even))
    far_across = swap_odd(rows((across,), to_odd))
    near_across = swap_even(rows((across,), to_even))
    rows2, fwd, inv3, back3 = [jnp.asarray(x) for x in tables()]
    spec, edge, energy = pl.pallas_call(
        functools.partial(early_kernel, tile_count),
        out_shape=(
            jax.ShapeDtypeStruct((4, QCOLS, HALF, 256), f32),
            jax.ShapeDtypeStruct((4, 2, QCOLS, 256), f32),
            jax.ShapeDtypeStruct((4, QCOLS, LANES), f32),
        ),
        in_specs=[vmem] * 7,
        out_specs=(vmem,) * 3,
        scratch_shapes=[pltpu.VMEM((4, PATCH, MSG), bf16), pltpu.VMEM((64, LANES), f32)],
        compiler_params=pltpu.CompilerParams(vmem_limit_bytes=24 * 1024 * 1024),
        name="early",
    )(eq, keep, sib, near_local, far_local, rows2, fwd)
    cells = pl.pallas_call(
        functools.partial(correlate_kernel, tile_count),
        out_shape=jax.ShapeDtypeStruct((FEATS, LANES), f32),
        in_specs=[pl.BlockSpec(memory_space=pl.ANY)] + [vmem] * 12,
        out_specs=vmem,
        scratch_shapes=[
            pltpu.VMEM((2, PATCH, MSG), bf16),
            pltpu.VMEM((6, QCOLS, HALF, 256), f32),
            pltpu.VMEM((6, 2, QCOLS, 256), f32),
            pltpu.VMEM((32, LANES), f32),
            pltpu.VMEM((6, QCOLS, LANES), f32),
            pltpu.VMEM((SECTIONS, QCOLS, HALF, 256), f32),
            pltpu.VMEM((2, QCOLS, PATCH, LANES), f32),
            pltpu.VMEM((QCOLS, FEATS, LANES), f32),
            pltpu.VMEM((SECTIONS, QCOLS, LANES), f32),
            pltpu.SMEM((SECTIONS,), jnp.int32),
            pltpu.SemaphoreType.DMA((4,)),
        ],
        compiler_params=pltpu.CompilerParams(vmem_limit_bytes=32 * 1024 * 1024),
        name="correlate",
    )(
        spec, edge, energy, keep, sib, across, far_across, near_across,
        patch_valid, rows2, fwd, inv3, back3,
    )
    cells = cells + lax.ppermute(cells, "sec", xor_route(SECTIONS, 1))
    cells = cells + swap(cells, perm=gather_route(tile_count, "z"))
    near = swap(cells, perm=gather_route(tile_count, "even"))
    far = swap(jnp.stack([cells, near]), perm=gather_route(tile_count, "odd"))
    third = swap(far[0], perm=gather_route(tile_count, "even"))
    bundle = jnp.stack([cells, near, far[0], far[1], third])
    shared = lax.ppermute(bundle, "sec", xor_route(SECTIONS, 1))
    return pl.pallas_call(
        functools.partial(relax_kernel, tile_count),
        out_shape=(
            jax.ShapeDtypeStruct((1, 2, 1, COLS), f32),
            jax.ShapeDtypeStruct((1, 1, COLS), f32),
            jax.ShapeDtypeStruct((1, 2, 1, COLS), f32),
        ),
        in_specs=[vmem] * 2,
        out_specs=(vmem,) * 3,
        compiler_params=pltpu.CompilerParams(vmem_limit_bytes=8 * 1024 * 1024),
        name="relax",
    )(bundle, shared)


def solution(mesh):
    in_specs = (P("sec", "tile", None), P(None, "tile", None), P("sec"), P("sec", "tile", None))
    out_specs = (P("sec", None, "tile", None), P("sec", "tile", None), P("sec", None, "tile", None))
    return jax.shard_map(
        per_device, mesh=mesh, in_specs=in_specs, out_specs=out_specs, check_vma=False
    )
```

```python
import functools
import math

import jax
import jax.numpy as jnp
import ml_dtypes
import numpy as np
from jax import lax
from jax.experimental import pallas as pl
from jax.experimental.pallas import tpu as pltpu
from jax.sharding import PartitionSpec as P

PATCH = 128
HALF = PATCH // 2
RIM = HALF // 2
STEPS = 3
SECTIONS = 4
COLS = 32
QCOLS = COLS // SECTIONS
QPIX = QCOLS * HALF
MSG = QPIX + PATCH
LANES = 128
FEATS = 16

score_scale = 800.0
spring_rate = 0.3
plane_weight = 0.5
f32 = jnp.float32
bf16 = jnp.bfloat16


def split_table(table):
    hi = table.astype(ml_dtypes.bfloat16)
    lo = (table - hi.astype(np.float64)).astype(ml_dtypes.bfloat16)
    return hi, lo


@functools.cache
def tables():
    n = np.arange(PATCH)
    angle = 2.0 * np.pi / PATCH * (np.outer(n, n) % PATCH)
    c, s = np.cos(angle), np.sin(angle)
    c[np.abs(c) < 1e-12] = 0.0
    s[np.abs(s) < 1e-12] = 0.0
    alt = (-1.0) ** n
    rows = np.concatenate([c[:HALF], alt[None], s[1:HALF]], axis=0)
    rows_hi, rows_lo = split_table(rows)
    rows2 = np.concatenate([rows_hi, rows_lo], axis=1)
    cols_cos = np.concatenate([c[:HALF], -s[:HALF]], axis=1)
    cols_sin = np.concatenate([-s[:HALF], -c[:HALF]], axis=1)
    even = np.concatenate([cols_cos, cols_sin], axis=0)
    odd = np.concatenate([cols_sin, cols_cos], axis=0) * np.concatenate([alt, alt])[None]
    even_hi, even_lo = split_table(even)
    odd_hi, odd_lo = split_table(odd)
    fwd = np.concatenate([even_hi, even_hi, even_lo, odd_hi, odd_hi, odd_lo], axis=0)
    inv = np.concatenate(
        [np.concatenate([c, s], axis=1), np.concatenate([-s, c], axis=1)], axis=0
    )
    inv_hi, inv_lo = split_table(inv)
    inv3 = np.concatenate([inv_hi, inv_hi, inv_lo], axis=0)
    back = np.concatenate([2.0 * c[:, :HALF], -2.0 * s[:, :HALF]], axis=1)
    back[:, 0] = 1.0
    back[:, HALF] = alt
    back_hi, back_lo = split_table(back / (PATCH * PATCH))
    back3 = np.concatenate([back_hi, back_hi, back_lo], axis=1)
    return (
        rows2,
        fwd,
        inv3,
        back3,
    )


def dot(a, b):
    return jnp.dot(a, b, preferred_element_type=f32)


def split(x):
    hi = x.astype(bf16)
    return hi, (x - hi.astype(f32)).astype(bf16)


def dot3(x, hi, lo):
    xh, xl = split(x)
    return dot(xh, hi) + dot(xl, hi) + dot(xh, lo)


def iota(shape, dim):
    return lax.broadcasted_iota(jnp.int32, shape, dim)


def prepare_kernel(strip, off, keep, send, wide):
    q = lax.axis_index("sec")
    h, c = lax.div(q, 2), lax.rem(q, 2)
    blank = jnp.zeros((HALF, LANES), bf16)
    wide[:, :LANES] = blank
    wide[:, LANES : LANES + COLS * HALF] = strip[0]
    wide[:, LANES + COLS * HALF :] = blank
    offset = jnp.broadcast_to(off[...].astype(f32), (HALF, MSG))
    marked = iota((HALF, MSG), 1) >= MSG - HALF
    for out, core in ((send, 1 - c), (keep, c)):
        for i, side in enumerate((h, 1 - h)):
            start = pl.multiple_of(QPIX * (2 * side + core), LANES)
            cut = wide[:, pl.ds(start, MSG + LANES)].astype(f32)
            cut = pltpu.roll(cut, MSG + RIM, 1)[:, :MSG]
            out[i] = jnp.where(marked, offset, cut).astype(bf16)


def place(x_ref, i, center, near, far, tile_count):
    t = lax.axis_index("tile")
    even = lax.rem(t, 2) == 0
    at_even = pl.multiple_of(jnp.where(even, PATCH - RIM, 0), RIM)
    at_odd = pl.multiple_of(jnp.where(even, 0, PATCH - RIM), RIM)
    no_odd = jnp.logical_or(t == 0, t == tile_count - 1)
    keep = jnp.where(no_odd, 0.0, 1.0).astype(bf16)
    x_ref[i, RIM : RIM + HALF, :] = center
    x_ref[i, pl.ds(at_even, RIM), :] = near
    x_ref[i, pl.ds(at_odd, RIM), :] = far * keep


def transform(x_ref, row0, count, rows2, fwd, spec_at, edge_at, energy_at):
    lane = iota((HALF, LANES), 1)
    low = lane < HALF
    window_row = iota((QCOLS, MSG), 0)
    window_lane = iota((QCOLS, MSG), 1)
    in_window = jnp.logical_and(
        window_lane >= window_row * HALF, window_lane < window_row * HALF + PATCH
    )
    for i in range(count):
        x = x_ref[i]
        xf = x.astype(f32)
        column = jnp.sum(xf * xf, axis=0, keepdims=True)
        windows = jnp.sum(jnp.where(in_window, column, 0.0), axis=1, keepdims=True)
        energy_at(i)[...] = jnp.broadcast_to(windows, (QCOLS, LANES))
        y = dot(rows2[...], jnp.concatenate([x, x], axis=0))
        evens, odds = [], []
        for v in range(QCOLS // 2 + 1):
            a = y[:HALF, LANES * v : LANES * (v + 1)]
            b = pltpu.roll(y[HALF:, LANES * v : LANES * (v + 1)], HALF, 1)
            g = jnp.where(low, a, b)
            evens.append(g)
            row0[16 * i + 2 * v : 16 * i + 2 * v + 1, :] = g[0:1]
            if v < QCOLS // 2:
                g = jnp.where(low, b, a)
                odds.append(g)
                row0[16 * i + 2 * v + 1 : 16 * i + 2 * v + 2, :] = pltpu.roll(g[0:1], HALF, 1)
        row0[16 * i + QCOLS + 1 : 16 * i + 16, :] = jnp.zeros((7, LANES), f32)
        gh, gl = split(jnp.concatenate(evens, axis=0))
        de = dot(jnp.concatenate([gh, gl, gh], axis=1), fwd[0:384])
        gh, gl = split(jnp.concatenate(odds, axis=0))
        do = dot(jnp.concatenate([gh, gl, gh], axis=1), fwd[384:768])
        for j in range(QCOLS):
            v = j // 2
            if j % 2 == 0:
                first, second = de[HALF * v : HALF * (v + 1)], do[HALF * v : HALF * (v + 1)]
            else:
                first, second = do[HALF * v : HALF * (v + 1)], de[HALF * (v + 1) : HALF * (v + 2)]
            spec_at(i)[j] = first + second
    edges = row0[...]
    edges = jnp.concatenate([edges, pltpu.roll(edges, HALF, 1)], axis=0)[:, :HALF]
    d0 = dot3(edges, fwd[0:HALF], fwd[256 : 256 + HALF])
    flip = (iota(d0.shape, 0) & iota(d0.shape, 1) & 1) == 1
    d0 = jnp.where(flip, -d0, d0)
    for i in range(count):
        for h in range(2):
            first = 16 * count * h + 16 * i
            edge_at(i)[h] = d0[first : first + QCOLS] + d0[first + 1 : first + QCOLS + 1]


def early_kernel(
    tile_count, eq, keep, sib, near, far, rows2, fwd, spec, edge, energy, x_ref, row0
):
    centers = [eq[0], eq[1], keep[0], sib[0]]
    for i, center in enumerate(centers):
        place(x_ref, i, center, near[i], far[i], tile_count)
    transform(
        x_ref, row0, 4, rows2, fwd,
        lambda i: spec.at[i], lambda i: edge.at[i], lambda i: energy.at[i],
    )


def correlate_kernel(
    tile_count,
    spec_in, edge_in, energy_in, keep, sib, across, far, near, valid,
    rows2, fwd, inv3, back3,
    out,
    x_ref, spec, spec0, row0, energy, u_ref, c_ref, part, peak, off_s, sems,
):
    q = lax.axis_index("sec")
    slots = [0, 1, q + 2, (q ^ 1) + 2, (q ^ 2) + 2, (q ^ 3) + 2]
    copies = [
        pltpu.make_async_copy(spec_in.at[i], spec.at[slots[i]], sems.at[i]) for i in range(4)
    ]
    for copy in copies:
        copy.start()
    for i in range(4):
        spec0[slots[i]] = edge_in[i]
        energy[slots[i]] = energy_in[i]
    for i, center in enumerate((keep.at[0], sib.at[0], across.at[0], across.at[1])):
        offset = jnp.max(center[:16, MSG - HALF :].astype(f32))
        off_s[slots[2 + i] - 2] = offset.astype(jnp.int32)
    for i in range(2):
        place(x_ref, i, across[i], near[i], far[i], tile_count)
    transform(
        x_ref, row0, 2, rows2, fwd,
        lambda i: spec.at[slots[4 + i]],
        lambda i: spec0.at[slots[4 + i]],
        lambda i: energy.at[slots[4 + i]],
    )

    prior = [s + 2 - off_s[s] for s in range(SECTIONS)]
    for copy in copies:
        copy.wait()

    lane1 = iota((1, LANES), 1)
    shift_lane = jnp.where(lane1 < HALF, lane1, lane1 - PATCH).astype(f32)
    sub8 = iota((8, LANES), 0).astype(f32)
    scales = []

    def inverse(s):
        prev = prior[s]
        scales.append(score_scale / jnp.sqrt(energy[s + 2] * energy[prev] + 1e-6))
        highs, lows = [], []
        for j in range(QCOLS):
            f, g = spec[s + 2, j], spec[prev, j]
            fr, fi = f[:, :PATCH], f[:, PATCH:]
            gr, gi = g[:, :PATCH], g[:, PATCH:]
            ph, plo = split(jnp.concatenate([fr * gr + fi * gi, fi * gr - fr * gi], axis=1))
            highs.append(ph)
            lows.append(plo)
        ph, plo = jnp.concatenate(highs, axis=0), jnp.concatenate(lows, axis=0)
        u = dot(jnp.concatenate([ph, plo, ph], axis=1), inv3[...])
        for j in range(QCOLS):
            u_ref[s, j] = u[HALF * j : HALF * (j + 1)]

    def edges():
        products = []
        for s in range(SECTIONS):
            for h in range(2):
                f, g = spec0[s + 2, h], spec0[prior[s], h]
                fr, fi = f[:, :PATCH], f[:, PATCH:]
                gr, gi = g[:, :PATCH], g[:, PATCH:]
                products.append(jnp.concatenate([fr * gr + fi * gi, fi * gr - fr * gi], axis=1))
        return dot3(
            jnp.concatenate(products, axis=0), inv3[0:256, 0:PATCH], inv3[512:768, 0:PATCH]
        )

    def patch_rows(s):
        first = 2 * QCOLS * s
        edge_rows = jnp.concatenate(
            [u0[first : first + QCOLS], u0[first + QCOLS : first + 2 * QCOLS]], axis=1
        )
        for j in range(QCOLS):
            u_ref[s, j, 0:1, :] = edge_rows[j : j + 1]

    def shifts(s):
        for j in range(0, QCOLS, 2):
            sides = []
            for k in (j, j + 1):
                uh, ul = split(u_ref[s, k])
                high = [uh[:, :PATCH], uh[:, PATCH:]]
                sides.append(
                    jnp.concatenate(high + [ul[:, :PATCH], ul[:, PATCH:]] + high, axis=0)
                )
            both = dot(back3[...], jnp.concatenate(sides, axis=1))
            for k in (j, j + 1):
                c = both[:, PATCH * (k - j) : PATCH * (k - j + 1)]
                c_ref[s % 2, k] = c
                peak[s, k : k + 1, :] = jnp.max(c, axis=0, keepdims=True)

    def soften(s):
        top8 = jnp.broadcast_to(jnp.max(peak[s], axis=1, keepdims=True), (QCOLS, LANES))
        peak[s] = top8
        rate8 = scales[s] * math.log2(math.e)
        for k in range(QCOLS):
            top = top8[k : k + 1, :]
            rate = rate8[k : k + 1, :]
            total = jnp.zeros((8, LANES), f32)
            moment = jnp.zeros((8, LANES), f32)
            for a in range(15, -1, -1):
                row = 8 * ((a + 8) % 16)
                total = total + jnp.exp2((c_ref[s % 2, k, row : row + 8, :] - top) * rate)
                if a:
                    moment = moment + total
            moment = 8.0 * moment + total * (sub8 - HALF)
            total = jnp.sum(total, axis=0, keepdims=True)
            part[k, s : s + 1, :] = jnp.sum(moment, axis=0, keepdims=True)
            part[k, 4 + s : 5 + s, :] = total * shift_lane
            part[k, 8 + s : 9 + s, :] = total

    inverse(0)
    u0 = edges()
    for s in range(SECTIONS):
        if s + 1 < SECTIONS:
            inverse(s + 1)
        patch_rows(s)
        shifts(s)
        if s:
            soften(s - 1)
    soften(SECTIONS - 1)

    lane16 = iota((FEATS, LANES), 1)
    lane4 = iota((SECTIONS, LANES), 1)
    lane8 = iota((QCOLS, LANES), 1)
    first_lane = q * QCOLS
    sums = jnp.zeros((FEATS, LANES), f32)
    for j in range(QCOLS):
        part[j, 12:16, :] = jnp.zeros((4, LANES), f32)
        sums = sums + jnp.where(
            lane16 == first_lane + j, jnp.sum(part[j], axis=1, keepdims=True), 0.0
        )
    pick = lane8 == first_lane + iota((QCOLS, LANES), 0)

    def gathered(rows):
        return jnp.concatenate(
            [jnp.sum(jnp.where(pick, x, 0.0), axis=0, keepdims=True) for x in rows], axis=0
        )

    rates = gathered(scales)
    tops = gathered([peak[s] for s in range(SECTIONS)])
    mine = jnp.logical_and(lane4 >= first_lane, lane4 < first_lane + QCOLS)
    total = jnp.where(mine, sums[8:12], 1.0)
    out[0:4, :] = sums[0:4] / total
    out[4:8, :] = sums[4:8] / total
    out[8:12, :] = jnp.where(mine, (tops * rates + jnp.log(total)) / score_scale, 0.0)
    row4 = iota((SECTIONS, LANES), 0)
    flags = jnp.concatenate(
        [
            valid[0].astype(f32),
            keep[0, 0:1, MSG - COLS :].astype(f32),
            jnp.zeros((1, HALF), f32),
        ],
        axis=1,
    )
    out[12:16, :] = jnp.where(row4 == q, flags, 0.0)


def relax_kernel(tile_count, mine, sib, flows_out, conf_out, pos_out):
    q = lax.axis_index("sec")
    t = lax.axis_index("tile")
    even = lax.rem(t, 2) == 0
    step = jnp.where(even, 1, -1)
    inside = lambda row: jnp.logical_and(row >= 0, row < tile_count)
    bundle = jnp.where(lax.rem(q, 2) == 1, mine[...], sib[...])
    own, near, far, beyond, third = [bundle[i] for i in range(5)]
    rows = [beyond, far, own, near, third]
    shape = (2 * SECTIONS, LANES)
    lane = iota(shape, 1)
    row = iota(shape, 0)
    sec = lax.rem(row, SECTIONS)
    live = lane < COLS
    offsets = jnp.max(
        jnp.where(iota((SECTIONS, LANES), 1) >= COLS, own[12:16], 0.0), axis=1, keepdims=True
    )
    offsets = jnp.broadcast_to(jnp.concatenate([offsets, offsets], axis=0), shape)
    one = offsets < 1.5
    flows, stiff, present = [], [], []
    for i, cells in enumerate(rows):
        ok = jnp.logical_and(live, inside(t + step * (i - 2)))
        present.append(ok)
        flows.append(jnp.where(ok, cells[0:8], 0.0))
        stiffness = cells[8:12] * cells[12:16]
        stiff.append(jnp.where(ok, jnp.concatenate([stiffness, stiffness], axis=0), 0.0))

    def back(x, n):
        return jnp.where(sec >= n, pltpu.roll(x, n, 0), 0.0)

    def ahead(x, n):
        return jnp.where(sec < SECTIONS - n, pltpu.roll(x, 2 * SECTIONS - n, 0), 0.0)

    zero = jnp.zeros(shape, f32)
    positions = [zero] * 5
    for iteration in range(STEPS):
        new = list(positions)
        for i in range(iteration, 5 - iteration):
            p = positions[i]
            if iteration == 0:
                tension = stiff[i] * flows[i]
                bending = zero
            else:
                pulled = jnp.where(one, back(p, 1), back(p, 2))
                tension = stiff[i] * (p - pulled + flows[i])
                bending = (
                    4.0 * p
                    - positions[i - 1]
                    - positions[i + 1]
                    - pltpu.roll(p, 1, 1)
                    - pltpu.roll(p, LANES - 1, 1)
                )
            returned = ahead(jnp.where(one, tension, 0.0), 1) + ahead(jnp.where(one, 0.0, tension), 2)
            gradient = tension - returned + plane_weight * bending
            new[i] = jnp.where(present[i], p - spring_rate * gradient, 0.0)
        positions = new
    for c in range(2):
        chosen = row == q + SECTIONS * c
        flows_out[0, c] = jnp.sum(jnp.where(chosen, flows[2], 0.0), axis=0, keepdims=True)[:, :COLS]
        pos_out[0, c] = jnp.sum(jnp.where(chosen, positions[2], 0.0), axis=0, keepdims=True)[:, :COLS]
    chosen = iota((SECTIONS, LANES), 0) == q
    conf_out[0] = jnp.sum(jnp.where(chosen, own[8:12], 0.0), axis=0, keepdims=True)[:, :COLS]


def xor_route(count, d):
    return [(i, i ^ d) for i in range(count)]


def joint_route(tile_count, odd):
    route = []
    for s in range(SECTIONS):
        for t in range(tile_count):
            to = t ^ 1 if not odd else t + (1 if t % 2 else -1)
            pair = (s, to) if 0 <= to < tile_count else (s ^ 1, t)
            route.append((s * tile_count + t, pair[0] * tile_count + pair[1]))
    return route


def gather_route(tile_count, kind):
    route = []
    for s in range(SECTIONS):
        for t in range(tile_count):
            pair = (s, t ^ 1)
            if s % 2 == 1 and kind == "z":
                pair = (s ^ 2, t)
            if s % 2 == 1 and kind == "odd":
                to = t + (1 if t % 2 else -1)
                pair = (s, to) if 0 <= to < tile_count else (s ^ 2, t)
            route.append((s * tile_count + t, pair[0] * tile_count + pair[1]))
    return route


def per_device(sections, earlier, offsets, patch_valid):
    tile_count = lax.axis_size("tile")
    q = lax.axis_index("sec")
    t = lax.axis_index("tile")
    even = t % 2 == 0
    swap = functools.partial(lax.ppermute, axis_name=("sec", "tile"))
    swap_even = functools.partial(swap, perm=joint_route(tile_count, False))
    swap_odd = functools.partial(swap, perm=joint_route(tile_count, True))
    vmem = pl.BlockSpec(memory_space=pltpu.VMEM)
    quarters = jax.ShapeDtypeStruct((2, HALF, MSG), bf16)
    keep, send = pl.pallas_call(
        prepare_kernel,
        out_shape=(quarters, quarters),
        in_specs=[vmem, vmem],
        out_specs=(vmem, vmem),
        scratch_shapes=[pltpu.VMEM((HALF, 2 * LANES + COLS * HALF), bf16)],
        compiler_params=pltpu.CompilerParams(vmem_limit_bytes=8 * 1024 * 1024),
        name="prepare",
    )(sections, offsets[None])
    sib = lax.ppermute(send, "sec", xor_route(SECTIONS, 1))
    across = lax.ppermute(jnp.stack([keep[1], sib[1]]), "sec", xor_route(SECTIONS, 2))
    right = QPIX * (SECTIONS - 1) + MSG - RIM - COLS * HALF
    eq = lax.dynamic_slice_in_dim(
        jnp.pad(earlier, ((0, 0), (0, 0), (RIM, right))), QPIX * q, MSG, axis=2
    )
    to_even = jnp.where(even, RIM, 0)
    to_odd = jnp.where(even, 0, RIM)

    def rows(images, start):
        return jnp.concatenate(
            [lax.dynamic_slice_in_dim(x, start, RIM, axis=1) for x in images], axis=0
        )

    local = (eq, keep[:1], sib[:1])
    far_local = swap_odd(rows(local, to_odd))
    near_local = swap_even(rows(local, to_even))
    far_across = swap_odd(rows((across,), to_odd))
    near_across = swap_even(rows((across,), to_even))
    rows2, fwd, inv3, back3 = [jnp.asarray(x) for x in tables()]
    spec, edge, energy = pl.pallas_call(
        functools.partial(early_kernel, tile_count),
        out_shape=(
            jax.ShapeDtypeStruct((4, QCOLS, HALF, 256), f32),
            jax.ShapeDtypeStruct((4, 2, QCOLS, 256), f32),
            jax.ShapeDtypeStruct((4, QCOLS, LANES), f32),
        ),
        in_specs=[vmem] * 7,
        out_specs=(vmem,) * 3,
        scratch_shapes=[pltpu.VMEM((4, PATCH, MSG), bf16), pltpu.VMEM((64, LANES), f32)],
        compiler_params=pltpu.CompilerParams(vmem_limit_bytes=24 * 1024 * 1024),
        name="early",
    )(eq, keep, sib, near_local, far_local, rows2, fwd)
    cells = pl.pallas_call(
        functools.partial(correlate_kernel, tile_count),
        out_shape=jax.ShapeDtypeStruct((FEATS, LANES), f32),
        in_specs=[pl.BlockSpec(memory_space=pl.ANY)] + [vmem] * 12,
        out_specs=vmem,
        scratch_shapes=[
            pltpu.VMEM((2, PATCH, MSG), bf16),
            pltpu.VMEM((6, QCOLS, HALF, 256), f32),
            pltpu.VMEM((6, 2, QCOLS, 256), f32),
            pltpu.VMEM((32, LANES), f32),
            pltpu.VMEM((6, QCOLS, LANES), f32),
            pltpu.VMEM((SECTIONS, QCOLS, HALF, 256), f32),
            pltpu.VMEM((2, QCOLS, PATCH, LANES), f32),
            pltpu.VMEM((QCOLS, FEATS, LANES), f32),
            pltpu.VMEM((SECTIONS, QCOLS, LANES), f32),
            pltpu.SMEM((SECTIONS,), jnp.int32),
            pltpu.SemaphoreType.DMA((4,)),
        ],
        compiler_params=pltpu.CompilerParams(vmem_limit_bytes=32 * 1024 * 1024),
        name="correlate",
    )(
        spec, edge, energy, keep, sib, across, far_across, near_across,
        patch_valid, rows2, fwd, inv3, back3,
    )
    cells = cells + lax.ppermute(cells, "sec", xor_route(SECTIONS, 1))
    cells = cells + swap(cells, perm=gather_route(tile_count, "z"))
    near = swap(cells, perm=gather_route(tile_count, "even"))
    far = swap(jnp.stack([cells, near]), perm=gather_route(tile_count, "odd"))
    third = swap(far[0], perm=gather_route(tile_count, "even"))
    bundle = jnp.stack([cells, near, far[0], far[1], third])
    shared = lax.ppermute(bundle, "sec", xor_route(SECTIONS, 1))
    return pl.pallas_call(
        functools.partial(relax_kernel, tile_count),
        out_shape=(
            jax.ShapeDtypeStruct((1, 2, 1, COLS), f32),
            jax.ShapeDtypeStruct((1, 1, COLS), f32),
            jax.ShapeDtypeStruct((1, 2, 1, COLS), f32),
        ),
        in_specs=[vmem] * 2,
        out_specs=(vmem,) * 3,
        compiler_params=pltpu.CompilerParams(vmem_limit_bytes=8 * 1024 * 1024),
        name="relax",
    )(bundle, shared)


def solution(mesh):
    in_specs = (P("sec", "tile", None), P(None, "tile", None), P("sec"), P("sec", "tile", None))
    out_specs = (P("sec", None, "tile", None), P("sec", "tile", None), P("sec", None, "tile", None))
    return jax.shard_map(
        per_device, mesh=mesh, in_specs=in_specs, out_specs=out_specs, check_vma=False
    )
```

```python
import functools
import math

import jax
import jax.numpy as jnp
import ml_dtypes
import numpy as np
from jax import lax
from jax.experimental import pallas as pl
from jax.experimental.pallas import tpu as pltpu
from jax.sharding import PartitionSpec as P

PATCH = 128
HALF = PATCH // 2
RIM = HALF // 2
STEPS = 3
SECTIONS = 4
COLS = 32
QCOLS = COLS // SECTIONS
QPIX = QCOLS * HALF
MSG = QPIX + PATCH
LANES = 128
FEATS = 16

score_scale = 800.0
spring_rate = 0.3
plane_weight = 0.5
f32 = jnp.float32
bf16 = jnp.bfloat16


def split_table(table):
    hi = table.astype(ml_dtypes.bfloat16)
    lo = (table - hi.astype(np.float64)).astype(ml_dtypes.bfloat16)
    return hi, lo


@functools.cache
def tables():
    n = np.arange(PATCH)
    angle = 2.0 * np.pi / PATCH * (np.outer(n, n) % PATCH)
    c, s = np.cos(angle), np.sin(angle)
    c[np.abs(c) < 1e-12] = 0.0
    s[np.abs(s) < 1e-12] = 0.0
    alt = (-1.0) ** n
    rows = np.concatenate([c[:HALF], alt[None], s[1:HALF]], axis=0)
    rows_hi, rows_lo = split_table(rows)
    rows2 = np.concatenate([rows_hi, rows_lo], axis=1)
    cols_cos = np.concatenate([c[:HALF], -s[:HALF]], axis=1)
    cols_sin = np.concatenate([-s[:HALF], -c[:HALF]], axis=1)
    even = np.concatenate([cols_cos, cols_sin], axis=0)
    odd = np.concatenate([cols_sin, cols_cos], axis=0) * np.concatenate([alt, alt])[None]
    even_hi, even_lo = split_table(even)
    odd_hi, odd_lo = split_table(odd)
    fwd = np.concatenate([even_hi, even_hi, even_lo, odd_hi, odd_hi, odd_lo], axis=0)
    inv = np.concatenate(
        [np.concatenate([c, s], axis=1), np.concatenate([-s, c], axis=1)], axis=0
    )
    inv_hi, inv_lo = split_table(inv)
    inv3 = np.concatenate([inv_hi, inv_hi, inv_lo], axis=0)
    back = np.concatenate([2.0 * c[:, :HALF], -2.0 * s[:, :HALF]], axis=1)
    back[:, 0] = 1.0
    back[:, HALF] = alt
    back_hi, back_lo = split_table(back / (PATCH * PATCH))
    back3 = np.concatenate([back_hi, back_hi, back_lo], axis=1)
    return (
        rows2,
        fwd,
        inv3,
        back3,
    )


def dot(a, b):
    return jnp.dot(a, b, preferred_element_type=f32)


def split(x):
    hi = x.astype(bf16)
    return hi, (x - hi.astype(f32)).astype(bf16)


def dot3(x, hi, lo):
    xh, xl = split(x)
    return dot(xh, hi) + dot(xl, hi) + dot(xh, lo)


def iota(shape, dim):
    return lax.broadcasted_iota(jnp.int32, shape, dim)


def prepare_kernel(strip, off, keep, send, wide):
    q = lax.axis_index("sec")
    h, c = lax.div(q, 2), lax.rem(q, 2)
    blank = jnp.zeros((HALF, LANES), bf16)
    wide[:, :LANES] = blank
    wide[:, LANES : LANES + COLS * HALF] = strip[0]
    wide[:, LANES + COLS * HALF :] = blank
    offset = jnp.broadcast_to(off[...].astype(f32), (HALF, MSG))
    marked = iota((HALF, MSG), 1) >= MSG - HALF
    for out, core in ((send, 1 - c), (keep, c)):
        for i, side in enumerate((h, 1 - h)):
            start = pl.multiple_of(QPIX * (2 * side + core), LANES)
            cut = wide[:, pl.ds(start, MSG + LANES)].astype(f32)
            cut = pltpu.roll(cut, MSG + RIM, 1)[:, :MSG]
            out[i] = jnp.where(marked, offset, cut).astype(bf16)


def place(x_ref, i, center, near, far, tile_count):
    t = lax.axis_index("tile")
    even = lax.rem(t, 2) == 0
    at_even = pl.multiple_of(jnp.where(even, PATCH - RIM, 0), RIM)
    at_odd = pl.multiple_of(jnp.where(even, 0, PATCH - RIM), RIM)
    no_odd = jnp.logical_or(t == 0, t == tile_count - 1)
    keep = jnp.where(no_odd, 0.0, 1.0).astype(bf16)
    x_ref[i, RIM : RIM + HALF, :] = center
    x_ref[i, pl.ds(at_even, RIM), :] = near
    x_ref[i, pl.ds(at_odd, RIM), :] = far * keep


def transform(x_ref, row0, count, rows2, fwd, spec_at, edge_at, energy_at):
    lane = iota((HALF, LANES), 1)
    low = lane < HALF
    window_row = iota((QCOLS, MSG), 0)
    window_lane = iota((QCOLS, MSG), 1)
    in_window = jnp.logical_and(
        window_lane >= window_row * HALF, window_lane < window_row * HALF + PATCH
    )
    for i in range(count):
        x = x_ref[i]
        xf = x.astype(f32)
        column = jnp.sum(xf * xf, axis=0, keepdims=True)
        windows = jnp.sum(jnp.where(in_window, column, 0.0), axis=1, keepdims=True)
        energy_at(i)[...] = jnp.broadcast_to(windows, (QCOLS, LANES))
        y = dot(rows2[...], jnp.concatenate([x, x], axis=0))
        evens, odds = [], []
        for v in range(QCOLS // 2 + 1):
            a = y[:HALF, LANES * v : LANES * (v + 1)]
            b = pltpu.roll(y[HALF:, LANES * v : LANES * (v + 1)], HALF, 1)
            g = jnp.where(low, a, b)
            evens.append(g)
            row0[16 * i + 2 * v : 16 * i + 2 * v + 1, :] = g[0:1]
            if v < QCOLS // 2:
                g = jnp.where(low, b, a)
                odds.append(g)
                row0[16 * i + 2 * v + 1 : 16 * i + 2 * v + 2, :] = pltpu.roll(g[0:1], HALF, 1)
        row0[16 * i + QCOLS + 1 : 16 * i + 16, :] = jnp.zeros((7, LANES), f32)
        gh, gl = split(jnp.concatenate(evens, axis=0))
        de = dot(jnp.concatenate([gh, gl, gh], axis=1), fwd[0:384])
        gh, gl = split(jnp.concatenate(odds, axis=0))
        do = dot(jnp.concatenate([gh, gl, gh], axis=1), fwd[384:768])
        for j in range(QCOLS):
            v = j // 2
            if j % 2 == 0:
                first, second = de[HALF * v : HALF * (v + 1)], do[HALF * v : HALF * (v + 1)]
            else:
                first, second = do[HALF * v : HALF * (v + 1)], de[HALF * (v + 1) : HALF * (v + 2)]
            spec_at(i)[j] = first + second
    edges = row0[...]
    edges = jnp.concatenate([edges, pltpu.roll(edges, HALF, 1)], axis=0)[:, :HALF]
    d0 = dot3(edges, fwd[0:HALF], fwd[256 : 256 + HALF])
    flip = (iota(d0.shape, 0) & iota(d0.shape, 1) & 1) == 1
    d0 = jnp.where(flip, -d0, d0)
    for i in range(count):
        for h in range(2):
            first = 16 * count * h + 16 * i
            edge_at(i)[h] = d0[first : first + QCOLS] + d0[first + 1 : first + QCOLS + 1]


def early_kernel(
    tile_count, eq, keep, sib, near, far, rows2, fwd, spec, edge, energy, x_ref, row0
):
    centers = [eq[0], eq[1], keep[0], sib[0]]
    for i, center in enumerate(centers):
        place(x_ref, i, center, near[i], far[i], tile_count)
    transform(
        x_ref, row0, 4, rows2, fwd,
        lambda i: spec.at[i], lambda i: edge.at[i], lambda i: energy.at[i],
    )


def correlate_kernel(
    tile_count,
    spec_in, edge_in, energy_in, keep, sib, across, far, near, valid,
    rows2, fwd, inv3, back3,
    out,
    x_ref, spec, spec0, row0, energy, u_ref, c_ref, part, peak, off_s, sems,
):
    q = lax.axis_index("sec")
    slots = [0, 1, q + 2, (q ^ 1) + 2, (q ^ 2) + 2, (q ^ 3) + 2]
    copies = [
        pltpu.make_async_copy(spec_in.at[i], spec.at[slots[i]], sems.at[i]) for i in range(4)
    ]
    for copy in copies:
        copy.start()
    for i in range(4):
        spec0[slots[i]] = edge_in[i]
        energy[slots[i]] = energy_in[i]
    for i, center in enumerate((keep.at[0], sib.at[0], across.at[0], across.at[1])):
        offset = jnp.max(center[:16, MSG - HALF :].astype(f32))
        off_s[slots[2 + i] - 2] = offset.astype(jnp.int32)
    for i in range(2):
        place(x_ref, i, across[i], near[i], far[i], tile_count)
    transform(
        x_ref, row0, 2, rows2, fwd,
        lambda i: spec.at[slots[4 + i]],
        lambda i: spec0.at[slots[4 + i]],
        lambda i: energy.at[slots[4 + i]],
    )

    prior = [s + 2 - off_s[s] for s in range(SECTIONS)]
    for copy in copies:
        copy.wait()

    lane1 = iota((1, LANES), 1)
    shift_lane = jnp.where(lane1 < HALF, lane1, lane1 - PATCH).astype(f32)
    sub8 = iota((8, LANES), 0).astype(f32)
    scales = []

    def inverse(s):
        prev = prior[s]
        scales.append(score_scale / jnp.sqrt(energy[s + 2] * energy[prev] + 1e-6))
        highs, lows = [], []
        for j in range(QCOLS):
            f, g = spec[s + 2, j], spec[prev, j]
            fr, fi = f[:, :PATCH], f[:, PATCH:]
            gr, gi = g[:, :PATCH], g[:, PATCH:]
            ph, plo = split(jnp.concatenate([fr * gr + fi * gi, fi * gr - fr * gi], axis=1))
            highs.append(ph)
            lows.append(plo)
        ph, plo = jnp.concatenate(highs, axis=0), jnp.concatenate(lows, axis=0)
        u = dot(jnp.concatenate([ph, plo, ph], axis=1), inv3[...])
        for j in range(QCOLS):
            u_ref[s, j] = u[HALF * j : HALF * (j + 1)]

    def edges():
        products = []
        for s in range(SECTIONS):
            for h in range(2):
                f, g = spec0[s + 2, h], spec0[prior[s], h]
                fr, fi = f[:, :PATCH], f[:, PATCH:]
                gr, gi = g[:, :PATCH], g[:, PATCH:]
                products.append(jnp.concatenate([fr * gr + fi * gi, fi * gr - fr * gi], axis=1))
        return dot3(
            jnp.concatenate(products, axis=0), inv3[0:256, 0:PATCH], inv3[512:768, 0:PATCH]
        )

    def patch_rows(s):
        first = 2 * QCOLS * s
        edge_rows = jnp.concatenate(
            [u0[first : first + QCOLS], u0[first + QCOLS : first + 2 * QCOLS]], axis=1
        )
        for j in range(QCOLS):
            u_ref[s, j, 0:1, :] = edge_rows[j : j + 1]

    def shifts(s):
        for j in range(0, QCOLS, 2):
            sides = []
            for k in (j, j + 1):
                uh, ul = split(u_ref[s, k])
                high = [uh[:, :PATCH], uh[:, PATCH:]]
                sides.append(
                    jnp.concatenate(high + [ul[:, :PATCH], ul[:, PATCH:]] + high, axis=0)
                )
            both = dot(back3[...], jnp.concatenate(sides, axis=1))
            for k in (j, j + 1):
                c = both[:, PATCH * (k - j) : PATCH * (k - j + 1)]
                c_ref[s % 2, k] = c
                peak[s, k : k + 1, :] = jnp.max(c, axis=0, keepdims=True)

    def soften(s):
        top8 = jnp.broadcast_to(jnp.max(peak[s], axis=1, keepdims=True), (QCOLS, LANES))
        peak[s] = top8
        rate8 = scales[s] * math.log2(math.e)
        for k in range(QCOLS):
            top = top8[k : k + 1, :]
            rate = rate8[k : k + 1, :]
            total = jnp.zeros((8, LANES), f32)
            moment = jnp.zeros((8, LANES), f32)
            for a in range(15, -1, -1):
                row = 8 * ((a + 8) % 16)
                total = total + jnp.exp2((c_ref[s % 2, k, row : row + 8, :] - top) * rate)
                if a:
                    moment = moment + total
            moment = 8.0 * moment + total * (sub8 - HALF)
            total = jnp.sum(total, axis=0, keepdims=True)
            part[k, s : s + 1, :] = jnp.sum(moment, axis=0, keepdims=True)
            part[k, 4 + s : 5 + s, :] = total * shift_lane
            part[k, 8 + s : 9 + s, :] = total

    inverse(0)
    inverse(1)
    u0 = edges()
    for s in range(SECTIONS):
        if 0 < s < SECTIONS - 1:
            inverse(s + 1)
        patch_rows(s)
        shifts(s)
        if s:
            soften(s - 1)
    soften(SECTIONS - 1)

    lane16 = iota((FEATS, LANES), 1)
    lane4 = iota((SECTIONS, LANES), 1)
    lane8 = iota((QCOLS, LANES), 1)
    first_lane = q * QCOLS
    sums = jnp.zeros((FEATS, LANES), f32)
    for j in range(QCOLS):
        part[j, 12:16, :] = jnp.zeros((4, LANES), f32)
        sums = sums + jnp.where(
            lane16 == first_lane + j, jnp.sum(part[j], axis=1, keepdims=True), 0.0
        )
    pick = lane8 == first_lane + iota((QCOLS, LANES), 0)

    def gathered(rows):
        return jnp.concatenate(
            [jnp.sum(jnp.where(pick, x, 0.0), axis=0, keepdims=True) for x in rows], axis=0
        )

    rates = gathered(scales)
    tops = gathered([peak[s] for s in range(SECTIONS)])
    mine = jnp.logical_and(lane4 >= first_lane, lane4 < first_lane + QCOLS)
    total = jnp.where(mine, sums[8:12], 1.0)
    out[0:4, :] = sums[0:4] / total
    out[4:8, :] = sums[4:8] / total
    out[8:12, :] = jnp.where(mine, (tops * rates + jnp.log(total)) / score_scale, 0.0)
    row4 = iota((SECTIONS, LANES), 0)
    flags = jnp.concatenate(
        [
            valid[0].astype(f32),
            keep[0, 0:1, MSG - COLS :].astype(f32),
            jnp.zeros((1, HALF), f32),
        ],
        axis=1,
    )
    out[12:16, :] = jnp.where(row4 == q, flags, 0.0)


def relax_kernel(tile_count, mine, sib, flows_out, conf_out, pos_out):
    q = lax.axis_index("sec")
    t = lax.axis_index("tile")
    even = lax.rem(t, 2) == 0
    step = jnp.where(even, 1, -1)
    inside = lambda row: jnp.logical_and(row >= 0, row < tile_count)
    bundle = jnp.where(lax.rem(q, 2) == 1, mine[...], sib[...])
    own, near, far, beyond, third = [bundle[i] for i in range(5)]
    rows = [beyond, far, own, near, third]
    shape = (2 * SECTIONS, LANES)
    lane = iota(shape, 1)
    row = iota(shape, 0)
    sec = lax.rem(row, SECTIONS)
    live = lane < COLS
    offsets = jnp.max(
        jnp.where(iota((SECTIONS, LANES), 1) >= COLS, own[12:16], 0.0), axis=1, keepdims=True
    )
    offsets = jnp.broadcast_to(jnp.concatenate([offsets, offsets], axis=0), shape)
    one = offsets < 1.5
    flows, stiff, present = [], [], []
    for i, cells in enumerate(rows):
        ok = jnp.logical_and(live, inside(t + step * (i - 2)))
        present.append(ok)
        flows.append(jnp.where(ok, cells[0:8], 0.0))
        stiffness = cells[8:12] * cells[12:16]
        stiff.append(jnp.where(ok, jnp.concatenate([stiffness, stiffness], axis=0), 0.0))

    def back(x, n):
        return jnp.where(sec >= n, pltpu.roll(x, n, 0), 0.0)

    def ahead(x, n):
        return jnp.where(sec < SECTIONS - n, pltpu.roll(x, 2 * SECTIONS - n, 0), 0.0)

    zero = jnp.zeros(shape, f32)
    positions = [zero] * 5
    for iteration in range(STEPS):
        new = list(positions)
        for i in range(iteration, 5 - iteration):
            p = positions[i]
            if iteration == 0:
                tension = stiff[i] * flows[i]
                bending = zero
            else:
                pulled = jnp.where(one, back(p, 1), back(p, 2))
                tension = stiff[i] * (p - pulled + flows[i])
                bending = (
                    4.0 * p
                    - positions[i - 1]
                    - positions[i + 1]
                    - pltpu.roll(p, 1, 1)
                    - pltpu.roll(p, LANES - 1, 1)
                )
            returned = ahead(jnp.where(one, tension, 0.0), 1) + ahead(jnp.where(one, 0.0, tension), 2)
            gradient = tension - returned + plane_weight * bending
            new[i] = jnp.where(present[i], p - spring_rate * gradient, 0.0)
        positions = new
    for c in range(2):
        chosen = row == q + SECTIONS * c
        flows_out[0, c] = jnp.sum(jnp.where(chosen, flows[2], 0.0), axis=0, keepdims=True)[:, :COLS]
        pos_out[0, c] = jnp.sum(jnp.where(chosen, positions[2], 0.0), axis=0, keepdims=True)[:, :COLS]
    chosen = iota((SECTIONS, LANES), 0) == q
    conf_out[0] = jnp.sum(jnp.where(chosen, own[8:12], 0.0), axis=0, keepdims=True)[:, :COLS]


def xor_route(count, d):
    return [(i, i ^ d) for i in range(count)]


def joint_route(tile_count, odd):
    route = []
    for s in range(SECTIONS):
        for t in range(tile_count):
            to = t ^ 1 if not odd else t + (1 if t % 2 else -1)
            pair = (s, to) if 0 <= to < tile_count else (s ^ 1, t)
            route.append((s * tile_count + t, pair[0] * tile_count + pair[1]))
    return route


def gather_route(tile_count, kind):
    route = []
    for s in range(SECTIONS):
        for t in range(tile_count):
            pair = (s, t ^ 1)
            if s % 2 == 1 and kind == "z":
                pair = (s ^ 2, t)
            if s % 2 == 1 and kind == "odd":
                to = t + (1 if t % 2 else -1)
                pair = (s, to) if 0 <= to < tile_count else (s ^ 2, t)
            route.append((s * tile_count + t, pair[0] * tile_count + pair[1]))
    return route


def per_device(sections, earlier, offsets, patch_valid):
    tile_count = lax.axis_size("tile")
    q = lax.axis_index("sec")
    t = lax.axis_index("tile")
    even = t % 2 == 0
    swap = functools.partial(lax.ppermute, axis_name=("sec", "tile"))
    swap_even = functools.partial(swap, perm=joint_route(tile_count, False))
    swap_odd = functools.partial(swap, perm=joint_route(tile_count, True))
    vmem = pl.BlockSpec(memory_space=pltpu.VMEM)
    quarters = jax.ShapeDtypeStruct((2, HALF, MSG), bf16)
    keep, send = pl.pallas_call(
        prepare_kernel,
        out_shape=(quarters, quarters),
        in_specs=[vmem, vmem],
        out_specs=(vmem, vmem),
        scratch_shapes=[pltpu.VMEM((HALF, 2 * LANES + COLS * HALF), bf16)],
        compiler_params=pltpu.CompilerParams(vmem_limit_bytes=8 * 1024 * 1024),
        name="prepare",
    )(sections, offsets[None])
    sib = lax.ppermute(send, "sec", xor_route(SECTIONS, 1))
    across = lax.ppermute(jnp.stack([keep[1], sib[1]]), "sec", xor_route(SECTIONS, 2))
    right = QPIX * (SECTIONS - 1) + MSG - RIM - COLS * HALF
    eq = lax.dynamic_slice_in_dim(
        jnp.pad(earlier, ((0, 0), (0, 0), (RIM, right))), QPIX * q, MSG, axis=2
    )
    to_even = jnp.where(even, RIM, 0)
    to_odd = jnp.where(even, 0, RIM)

    def rows(images, start):
        return jnp.concatenate(
            [lax.dynamic_slice_in_dim(x, start, RIM, axis=1) for x in images], axis=0
        )

    local = (eq, keep[:1], sib[:1])
    far_local = swap_odd(rows(local, to_odd))
    near_local = swap_even(rows(local, to_even))
    far_across = swap_odd(rows((across,), to_odd))
    near_across = swap_even(rows((across,), to_even))
    rows2, fwd, inv3, back3 = [jnp.asarray(x) for x in tables()]
    spec, edge, energy = pl.pallas_call(
        functools.partial(early_kernel, tile_count),
        out_shape=(
            jax.ShapeDtypeStruct((4, QCOLS, HALF, 256), f32),
            jax.ShapeDtypeStruct((4, 2, QCOLS, 256), f32),
            jax.ShapeDtypeStruct((4, QCOLS, LANES), f32),
        ),
        in_specs=[vmem] * 7,
        out_specs=(vmem,) * 3,
        scratch_shapes=[pltpu.VMEM((4, PATCH, MSG), bf16), pltpu.VMEM((64, LANES), f32)],
        compiler_params=pltpu.CompilerParams(vmem_limit_bytes=24 * 1024 * 1024),
        name="early",
    )(eq, keep, sib, near_local, far_local, rows2, fwd)
    cells = pl.pallas_call(
        functools.partial(correlate_kernel, tile_count),
        out_shape=jax.ShapeDtypeStruct((FEATS, LANES), f32),
        in_specs=[pl.BlockSpec(memory_space=pl.ANY)] + [vmem] * 12,
        out_specs=vmem,
        scratch_shapes=[
            pltpu.VMEM((2, PATCH, MSG), bf16),
            pltpu.VMEM((6, QCOLS, HALF, 256), f32),
            pltpu.VMEM((6, 2, QCOLS, 256), f32),
            pltpu.VMEM((32, LANES), f32),
            pltpu.VMEM((6, QCOLS, LANES), f32),
            pltpu.VMEM((SECTIONS, QCOLS, HALF, 256), f32),
            pltpu.VMEM((2, QCOLS, PATCH, LANES), f32),
            pltpu.VMEM((QCOLS, FEATS, LANES), f32),
            pltpu.VMEM((SECTIONS, QCOLS, LANES), f32),
            pltpu.SMEM((SECTIONS,), jnp.int32),
            pltpu.SemaphoreType.DMA((4,)),
        ],
        compiler_params=pltpu.CompilerParams(vmem_limit_bytes=32 * 1024 * 1024),
        name="correlate",
    )(
        spec, edge, energy, keep, sib, across, far_across, near_across,
        patch_valid, rows2, fwd, inv3, back3,
    )
    cells = cells + lax.ppermute(cells, "sec", xor_route(SECTIONS, 1))
    cells = cells + swap(cells, perm=gather_route(tile_count, "z"))
    near = swap(cells, perm=gather_route(tile_count, "even"))
    far = swap(jnp.stack([cells, near]), perm=gather_route(tile_count, "odd"))
    third = swap(far[0], perm=gather_route(tile_count, "even"))
    bundle = jnp.stack([cells, near, far[0], far[1], third])
    shared = lax.ppermute(bundle, "sec", xor_route(SECTIONS, 1))
    return pl.pallas_call(
        functools.partial(relax_kernel, tile_count),
        out_shape=(
            jax.ShapeDtypeStruct((1, 2, 1, COLS), f32),
            jax.ShapeDtypeStruct((1, 1, COLS), f32),
            jax.ShapeDtypeStruct((1, 2, 1, COLS), f32),
        ),
        in_specs=[vmem] * 2,
        out_specs=(vmem,) * 3,
        compiler_params=pltpu.CompilerParams(vmem_limit_bytes=8 * 1024 * 1024),
        name="relax",
    )(bundle, shared)


def solution(mesh):
    in_specs = (P("sec", "tile", None), P(None, "tile", None), P("sec"), P("sec", "tile", None))
    out_specs = (P("sec", None, "tile", None), P("sec", "tile", None), P("sec", None, "tile", None))
    return jax.shard_map(
        per_device, mesh=mesh, in_specs=in_specs, out_specs=out_specs, check_vma=False
    )
```
